128 devices in a mesh: row: 16 (over z_lo, y, core), cand: 8 (over z_hi, x).
Axes of the slice: x: 4, y: 4, z: 4 (z_hi: 2, z_lo: 2; z = z_hi * 2 + z_lo), core: 2. Of those that a mesh axis runs over, the one named last changes fastest.
Arguments:
- embeddings: bfloat16 [131072, 768], P('row')
- pick_index: int32 [64], replicated, may hold values from 0 to 131071
- cand_index: int32 [8192], replicated, may hold values from 0 to 131071
Outputs:
- gains: float32 [8192], P('cand')
- coverage: float32 [131072], P('row')
The draws below stay inside these ranges and needn't reach their ends.
All inputs are finite; a program needn't handle non-finite values.
Results may differ from the reference program's by a relative error of at most 0.0003.
Values may be sent and summed in bfloat16 or wider, within the bound.
A program may use at most 128 MiB of HBM per device.

```python
import jax
import jax.numpy as jnp
from jax import lax

D = 768
ROW_DEV = 8192
NPICK = 64
ROWS = 131072
CAND = 8192


def draw_embeddings(key, part):
    key = jax.random.fold_in(key, 7)
    key_noise, key_row, key_col, key_centre = jax.random.split(key, 4)
    run_length = max(1, 4 * ROW_DEV // 256)
    cluster_of = jnp.arange(ROWS, dtype=jnp.int32) // run_length % 256
    own_part = jax.random.normal(key_noise, (ROWS, D), jnp.float32)
    centres = jax.random.normal(key_centre, (256, D), jnp.float32)
    mixture = 0.9 * centres[cluster_of] + 0.45 * own_part
    position = jnp.arange(ROWS, dtype=jnp.float32) / ROWS
    row_scale = jnp.exp(jnp.log(3.0) * position) * jnp.exp(jax.random.uniform(key_row, (ROWS,), jnp.float32, 0.0, jnp.log(3.0)))
    col_scale = jnp.exp(jax.random.uniform(key_col, (D,), jnp.float32, jnp.log(0.5), jnp.log(2.0)))
    values = mixture * row_scale[:, None] * col_scale[None, :] * D ** (-0.25) / 3.0
    return values.astype(jnp.bfloat16)


def set_ends(result, key, low, largest):
    shape = result.shape
    index_at = [jax.random.randint(jax.random.fold_in(key, axis), (), 0, shape[axis]) for axis in range(len(shape))]
    result = result.at[tuple(index_at)].set(low)
    longest = shape.index(max(shape))
    index_at[longest] = (index_at[longest] + 1) % shape[longest]
    return result.at[tuple(index_at)].set(largest)


def setup_inputs(seed: int = 0) -> dict:
    streams_of = jax.random.split(jax.random.key(seed), 4)
    return {
        "embeddings": draw_embeddings(jax.random.fold_in(streams_of[3], 71), 0),
        "pick_index": set_ends(jax.random.randint(streams_of[1], (NPICK,), 0, ROWS), jax.random.fold_in(streams_of[1], 1), 0, ROWS - 1).astype(jnp.int32),
        "cand_index": set_ends(jax.random.randint(streams_of[2], (CAND,), 0, ROWS), jax.random.fold_in(streams_of[2], 1), 0, ROWS - 1).astype(jnp.int32),
    }


def reference(embeddings, pick_index, cand_index):
    picked = embeddings[pick_index]
    chosen = embeddings[cand_index]
    block = min(4096, ROWS)
    blocks = embeddings.reshape(ROWS // block, block, D)

    def one_block(rows):
        cover = jnp.max(lax.dot_general(rows, picked, (((1,), (1,)), ((), ())), preferred_element_type=jnp.float32), axis=1)
        similar = lax.dot_general(rows, chosen, (((1,), (1,)), ((), ())), preferred_element_type=jnp.float32)
        return cover, jnp.sum(jnp.maximum(similar - cover[:, None], 0.0), axis=0)

    covers, partial_value = lax.map(one_block, blocks)
    gains = jnp.sum(partial_value, axis=0) / ROWS
    return gains, covers.reshape(ROWS)
```

```python
import functools

import jax
import jax.numpy as jnp
from jax import lax
from jax.experimental import pallas as pl
from jax.experimental.pallas import tpu as pltpu
from jax.sharding import PartitionSpec as P

MESH = pl.DeviceIdType.MESH
F32 = jnp.float32
BF16 = jnp.bfloat16

CHIPS = ((0, 0), (1, 0), (0, 1), (0, 3), (1, 1), (1, 3), (0, 2), (1, 2))
ORDER = tuple((dz, dy, dc) for dz, dy in CHIPS for dc in (0, 1))
SLOT = {rel: j for j, rel in enumerate(ORDER)}
OWNERS = 16
CAP = 96
PCAP = 16
TILES = ((0, 192, 0, 4), (192, 432, 2, 8), (432, 704, 5, 12), (704, 1024, 9, 16))
PER = 1024
PICKS = 64


def iota(shape, dim):
    return lax.broadcasted_iota(jnp.int32, shape, dim)


def dot(a, b):
    return jnp.dot(a, b, preferred_element_type=F32)


def inner(left, right):
    return lax.dot_general(left, right, (((1,), (1,)), ((), ())), preferred_element_type=F32)


def ones_where(cond):
    return jnp.where(cond, 1.0, 0.0).astype(BF16)


def order_of(owner, device):
    dz = (owner >> 3) ^ (device >> 3)
    dy = ((owner >> 1) - (device >> 1)) & 3
    chip = dz * 4 + dy
    place = jnp.zeros_like(chip)
    for rank, (cz, cy) in enumerate(CHIPS):
        place = jnp.where(chip == cz * 4 + cy, rank, place)
    return place * 2 + ((owner ^ device) & 1)


def kernel(
    block_rows, shift,
    cand_ref, pick_ref, pick_col_ref, emb_hbm,
    gains_ref, cover_ref, flag_ref,
    emb, blk, pk, ch, acc, red,
    load_sem, pk_send, pk_recv, blk_send, blk_recv, red_send, red_recv,
):
    rows = emb.shape[0]
    chunks = load_sem.shape[0]
    chunk = rows // chunks
    me = lax.axis_index("row")
    group = lax.axis_index("cand")
    z, y, c = me // 8, (me // 2) % 4, me % 2

    def device(dz, dy, dc):
        return (z + dz) % 2 * 8 + (y + dy) % 4 * 2 + (c + dc) % 2

    def load(i):
        at = pl.ds(pl.multiple_of(i * chunk, chunk), chunk)
        return pltpu.make_async_copy(emb_hbm.at[at], emb.at[at], load_sem.at[i])

    for i in range(chunks):
        load(i).start()

    barrier = pltpu.get_barrier_semaphore()
    for rel in ORDER[1:]:
        pl.semaphore_signal(barrier, inc=1, device_id={"row": device(*rel)}, device_id_type=MESH)

    mine = cand_ref[pl.ds(pl.multiple_of(group * 8, 8), 8), :]
    owner, local = mine >> shift, mine & (rows - 1)
    masks = [owner == device(*rel) for rel in ORDER]
    mask = jnp.concatenate([jnp.where(m, 1.0, 0.0) for m in masks], axis=0).astype(BF16)
    r0, r1 = iota((128, 128), 0), iota((128, 128), 1)
    before = ones_where(r0 < r1)
    within = dot(mask, before)
    totals = dot(mask, jnp.ones((128, 128), BF16)).astype(BF16)
    same = (r0 >> 3) == (r1 >> 3)
    rank = within + dot(ones_where(same & (r1 < r0)), totals)
    count = dot(ones_where(same), totals)
    base = dot(ones_where((r1 >> 3) < (r0 >> 3)), totals)
    place = jnp.zeros((8, 128), F32)
    for j in range(OWNERS):
        at = slice(8 * j, 8 * j + 8)
        place += jnp.where(masks[j], rank[at] + base[at], 0.0)

    key = jnp.where(masks[0], rank[:8], -1.0)
    local_plus = (local + 1).astype(F32)
    slot_row = jnp.zeros((CAP, 128), F32)
    slots = iota((CAP, 128), 0).astype(F32)
    for r in range(8):
        slot_row += jnp.where(slots == key[r:r + 1], local_plus[r:r + 1], 0.0)
    cand_at = jnp.sum(slot_row, axis=1, keepdims=True)
    pick = pick_ref[...]
    pick_mine = jnp.broadcast_to((pick >> shift) == me, (8, 128))
    pick_rank = dot(ones_where(pick_mine), before)
    pick_key = jnp.where(pick_mine, pick_rank, -1.0)
    pick_plus = ((pick & (rows - 1)) + 1).astype(F32)
    pick_at = jnp.sum(
        jnp.where(iota((PCAP, 128), 0).astype(F32) == pick_key[:1], pick_plus, 0.0),
        axis=1, keepdims=True)
    at_row = jnp.concatenate([cand_at, pick_at], axis=0).astype(jnp.int32) - 1
    at_row = jnp.broadcast_to(at_row, (CAP + PCAP, chunk))

    lanes = iota((CAP + PCAP, chunk), 1)

    def gather(i, total):
        load(i).wait()
        at = pl.ds(pl.multiple_of(i * chunk, chunk), chunk)
        return total + dot(ones_where(at_row - i * chunk == lanes), emb[at, :])

    total = lax.fori_loop(0, chunks, gather, jnp.zeros((CAP + PCAP, emb.shape[1]), F32))
    pk[0] = total[CAP:].astype(BF16)
    blk[0] = total[:CAP].astype(BF16)

    pl.semaphore_wait(barrier, OWNERS - 1)

    def send(buf, src, dst, send_sem, recv_sem, rel):
        return pltpu.make_async_remote_copy(
            src_ref=buf.at[src], dst_ref=buf.at[dst], send_sem=send_sem, recv_sem=recv_sem.at[dst],
            device_id={"row": device(*rel)}, device_id_type=MESH)

    def send_own(buf, send_sems, recv_sems, rel):
        dz, dy, dc = rel
        return send(buf, 0, SLOT[dz, -dy % 4, dc], send_sems.at[SLOT[rel]], recv_sems, rel)

    def forward(j):
        dz, dy, _ = ORDER[j]
        return send(blk, j, SLOT[dz, dy, 1], blk_send.at[SLOT[dz, dy, 1]], blk_recv, (0, 0, 1))

    for rel in ORDER[1:]:
        send_own(pk, pk_send, pk_recv, rel).start()
    for rel in ORDER[1:]:
        if rel[2] == 0 or rel == (0, 0, 1):
            send_own(blk, blk_send, blk_recv, rel).start()

    def wait_block(j):
        dz, dy, dc = ORDER[j]
        send(blk, 0, j, blk_send.at[j], blk_recv, (0, 0, 1)).wait_recv()

    held = jnp.zeros((8, 128), F32)
    every = cand_ref[...] >> shift
    for o in range(OWNERS):
        hit = jnp.where(every == o, 1.0, 0.0).reshape(8, 8, 128).sum(axis=1)
        held = jnp.where(iota((8, 128), 1) == o, jnp.sum(hit, axis=1, keepdims=True), held)
    lane = iota((128, 128), 1)
    limits = [(hi, last, 1) for _, hi, _, last in TILES[:-1]] + [(lo, first, 0) for lo, _, first, _ in TILES[1:]]
    which = lane >> 4
    window = jnp.zeros((128, 128), jnp.int32)
    for k, (_, edge, _) in enumerate(limits):
        window = jnp.where(which == k, edge, window)
    prefix = ones_where((order_of(iota((128, 128), 0), lane & 15) < window) & (iota((128, 128), 0) < OWNERS))
    sums = dot(held.astype(BF16), prefix)
    bad = held > CAP
    for k, (bound, _, least) in enumerate(limits):
        off = sums < bound if least else sums > bound
        bad = bad | ((which[:8] == k) & off)
    pick_col = pick_col_ref[...] >> shift
    pick_hit = jnp.where(pick_col == iota((PICKS, 128), 1), 1.0, 0.0)
    pick_over = jnp.sum(pick_hit, axis=0, keepdims=True) > PCAP
    worst = jnp.maximum(jnp.max(jnp.where(bad, 1.0, 0.0)), jnp.max(jnp.where(pick_over, 1.0, 0.0)))
    flag_ref[0, 0] = worst.astype(jnp.int32)

    pick_order = order_of(pick_col, me)
    pick_one = ones_where(pick_order == iota((PICKS, 128), 1))
    earlier = dot(ones_where(iota((PICKS, PICKS), 1) < iota((PICKS, PICKS), 0)), pick_one)
    pick_rank_col = jnp.sum(jnp.where(pick_order == iota((PICKS, 128), 1), earlier, 0.0), axis=1, keepdims=True)
    pick_slot = pick_order[:, :1] * PCAP + pick_rank_col.astype(jnp.int32)
    for j in range(1, OWNERS):
        send(pk, 0, j, pk_send.at[j], pk_recv, (0, 0, 1)).wait_recv()
    picked = dot(
        ones_where(pick_slot == iota((PICKS, OWNERS * PCAP), 1)),
        pk[...].reshape(OWNERS * PCAP, emb.shape[1]))
    ch[:PICKS] = picked.astype(BF16)

    seen = {0}
    for t, (lo, hi, first, last) in enumerate(TILES):
        for j in range(last):
            if j not in seen and ORDER[j][2] == 0:
                wait_block(j)
                forward(j).start()
        for j in range(last):
            if j not in seen and ORDER[j][2] == 1:
                wait_block(j)
            seen.add(j)
        dense = jnp.zeros((hi - lo, emb.shape[1]), F32)
        for j in range(first, last):
            row = iota((hi - lo, CAP), 0) + lo
            slot = iota((hi - lo, CAP), 1)
            start = base[8 * j:8 * j + 1, :CAP].astype(jnp.int32)
            held_j = count[8 * j:8 * j + 1, :CAP].astype(jnp.int32)
            dense += dot(ones_where((row == start + slot) & (slot < held_j)), blk[j])
        ch[PICKS + lo:PICKS + hi] = dense.astype(BF16)
        acc[lo:hi] = jnp.zeros((hi - lo, 128), F32)

        def step(i, carry, t=t, lo=lo, hi=hi):
            e = emb[pl.ds(pl.multiple_of(i * block_rows, block_rows), block_rows), :]
            if t == 0:
                s = inner(ch[:PICKS + hi], e)
                cover = jnp.max(s[:PICKS], axis=0, keepdims=True)
                s = s[PICKS:]
            else:
                s = inner(ch[PICKS + lo:PICKS + hi], e)
            part = acc[lo:hi]
            for k in range(block_rows // 128):
                at = pl.ds(i * (block_rows // 128) + k, 1)
                lanes_k = slice(128 * k, 128 * k + 128)
                if t == 0:
                    cover_k = cover[:, lanes_k]
                    cover_ref[at, :] = cover_k
                else:
                    cover_k = cover_ref[at, :]
                part += jnp.maximum(s[:, lanes_k] - cover_k, 0.0)
            acc[lo:hi] = part
            return carry

        lax.fori_loop(0, rows // block_rows, step, 0)

    found = jnp.sum(acc[...], axis=1, keepdims=True)
    dense_at = iota((PER, 128), 0).astype(F32)
    parts = []
    for r in range(8):
        parts.append(jnp.sum(jnp.where(dense_at == place[r:r + 1], found, 0.0), axis=0, keepdims=True))
    red[me] = jnp.concatenate(parts, axis=0)

    def share(rel):
        return pltpu.make_async_remote_copy(
            src_ref=red.at[me], dst_ref=red.at[me], send_sem=red_send.at[SLOT[rel]], recv_sem=red_recv.at[me],
            device_id={"row": device(*rel)}, device_id_type=MESH)

    for rel in ORDER[1:]:
        share(rel).start()
    for rel in ORDER[1:]:
        o = device(*rel)
        pltpu.make_async_remote_copy(
            src_ref=red.at[me], dst_ref=red.at[o], send_sem=red_send.at[SLOT[rel]], recv_sem=red_recv.at[o],
            device_id={"row": o}, device_id_type=MESH).wait_recv()
    whole = red[0]
    for o in range(1, OWNERS):
        whole += red[o]
    gains_ref[...] = whole * (1.0 / (rows * OWNERS))

    for rel in ORDER[1:]:
        send_own(pk, pk_send, pk_recv, rel).wait_send()
        share(rel).wait_send()
        if rel[2] == 0 or rel == (0, 0, 1):
            send_own(blk, blk_send, blk_recv, rel).wait_send()
        if rel[2] == 0:
            forward(SLOT[rel]).wait_send()


def select_owned(embeddings, indices):
    count = embeddings.shape[0]
    local = indices - lax.axis_index("row") * count
    owned = (local >= 0) & (local < count)
    taken = jnp.take(embeddings, jnp.clip(local, 0, count - 1), axis=0)
    return jnp.where(owned[:, None], taken, jnp.zeros_like(taken))


def whole_path(embeddings, pick_index, cand_index):
    count = embeddings.shape[0]
    per = cand_index.shape[0] // lax.axis_size("cand")
    mine = lax.dynamic_slice_in_dim(cand_index, lax.axis_index("cand") * per, per, 0)
    picked = lax.psum(select_owned(embeddings, pick_index), "row")
    coverage = jnp.max(inner(embeddings, picked), axis=1)
    chosen = lax.psum(select_owned(embeddings, mine), "row")
    similar = inner(embeddings, chosen)
    partial = jnp.sum(jnp.maximum(similar - coverage[:, None], 0.0), axis=0)
    return lax.psum(partial, "row") / (count * lax.axis_size("row")), coverage


def per_device(embeddings, pick_index, cand_index):
    rows, width = embeddings.shape
    shift = rows.bit_length() - 1
    chunks = 8
    block_rows = 2048
    pick_row = jnp.concatenate([pick_index, jnp.full((128 - PICKS,), -1, jnp.int32)]).reshape(1, 128)
    vmem = pl.BlockSpec(memory_space=pltpu.VMEM)
    gains, cover, flag = pl.pallas_call(
        functools.partial(kernel, block_rows, shift),
        out_shape=[
            jax.ShapeDtypeStruct((8, 128), F32),
            jax.ShapeDtypeStruct((rows // 128, 128), F32),
            jax.ShapeDtypeStruct((1, 1), jnp.int32),
        ],
        in_specs=[vmem, vmem, vmem, pl.BlockSpec(memory_space=pl.ANY)],
        out_specs=[vmem, vmem, pl.BlockSpec(memory_space=pltpu.SMEM)],
        scratch_shapes=[
            pltpu.VMEM((rows, width), BF16),
            pltpu.VMEM((OWNERS, CAP, width), BF16),
            pltpu.VMEM((OWNERS, PCAP, width), BF16),
            pltpu.VMEM((PICKS + PER, width), BF16),
            pltpu.VMEM((PER, 128), F32),
            pltpu.VMEM((OWNERS, 8, 128), F32),
            pltpu.SemaphoreType.DMA((chunks,)),
            pltpu.SemaphoreType.DMA((OWNERS,)),
            pltpu.SemaphoreType.DMA((OWNERS,)),
            pltpu.SemaphoreType.DMA((OWNERS,)),
            pltpu.SemaphoreType.DMA((OWNERS,)),
            pltpu.SemaphoreType.DMA((OWNERS,)),
            pltpu.SemaphoreType.DMA((OWNERS,)),
        ],
        compiler_params=pltpu.CompilerParams(
            collective_id=0, has_side_effects=True, vmem_limit_bytes=60 * 2**20),
        cost_estimate=pl.CostEstimate(
            flops=2 * rows * (PER + PICKS) * width, bytes_accessed=2 * rows * width, transcendentals=0),
    )(cand_index.reshape(-1, 128), pick_row, pick_index.reshape(PICKS, 1), embeddings)
    return lax.cond(
        flag[0, 0] == 0,
        lambda: (gains.reshape(PER), cover.reshape(rows)),
        lambda: whole_path(embeddings, pick_index, cand_index),
    )


def solution(mesh):
    return jax.shard_map(
        per_device,
        mesh=mesh,
        in_specs=(P("row", None), P(), P()),
        out_specs=(P("cand"), P("row")),
        check_vma=False,
    )
```

```python
import functools

import jax
import jax.numpy as jnp
from jax import lax
from jax.experimental import pallas as pl
from jax.experimental.pallas import tpu as pltpu
from jax.sharding import PartitionSpec as P

MESH = pl.DeviceIdType.MESH
F32 = jnp.float32
BF16 = jnp.bfloat16

CHIPS = ((0, 0), (1, 0), (0, 1), (0, 3), (1, 1), (1, 3), (0, 2), (1, 2))
ORDER = tuple((dz, dy, dc) for dz, dy in CHIPS for dc in (0, 1))
SLOT = {rel: j for j, rel in enumerate(ORDER)}
OWNERS = 16
CAP = 96
PCAP = 16
TILES = ((0, 192, 0, 4), (192, 432, 2, 8), (432, 704, 5, 12), (704, 1024, 9, 16))
PER = 1024
PICKS = 64


def iota(shape, dim):
    return lax.broadcasted_iota(jnp.int32, shape, dim)


def dot(a, b):
    return jnp.dot(a, b, preferred_element_type=F32)


def inner(left, right):
    return lax.dot_general(left, right, (((1,), (1,)), ((), ())), preferred_element_type=F32)


def ones_where(cond):
    return jnp.where(cond, 1.0, 0.0).astype(BF16)


def order_of(owner, device):
    dz = (owner >> 3) ^ (device >> 3)
    dy = ((owner >> 1) - (device >> 1)) & 3
    chip = dz * 4 + dy
    place = jnp.zeros_like(chip)
    for rank, (cz, cy) in enumerate(CHIPS):
        place = jnp.where(chip == cz * 4 + cy, rank, place)
    return place * 2 + ((owner ^ device) & 1)


def kernel(
    block_rows, shift,
    cand_ref, pick_ref, pick_col_ref, emb_hbm,
    gains_ref, cover_ref, flag_ref,
    emb, blk, pk, ch, acc, red,
    load_sem, pk_send, pk_recv, blk_send, blk_recv, red_send, red_recv,
):
    rows = emb.shape[0]
    chunks = load_sem.shape[0]
    chunk = rows // chunks
    me = lax.axis_index("row")
    group = lax.axis_index("cand")
    z, y, c = me // 8, (me // 2) % 4, me % 2

    def device(dz, dy, dc):
        return (z + dz) % 2 * 8 + (y + dy) % 4 * 2 + (c + dc) % 2

    def load(i):
        at = pl.ds(pl.multiple_of(i * chunk, chunk), chunk)
        return pltpu.make_async_copy(emb_hbm.at[at], emb.at[at], load_sem.at[i])

    for i in range(chunks):
        load(i).start()

    barrier = pltpu.get_barrier_semaphore()
    for rel in ORDER[1:]:
        pl.semaphore_signal(barrier, inc=1, device_id={"row": device(*rel)}, device_id_type=MESH)

    mine = cand_ref[pl.ds(pl.multiple_of(group * 8, 8), 8), :]
    owner, local = mine >> shift, mine & (rows - 1)
    masks = [owner == device(*rel) for rel in ORDER]
    mask = jnp.concatenate([jnp.where(m, 1.0, 0.0) for m in masks], axis=0).astype(BF16)
    r0, r1 = iota((128, 128), 0), iota((128, 128), 1)
    before = ones_where(r0 < r1)
    within = dot(mask, before)
    totals = dot(mask, jnp.ones((128, 128), BF16)).astype(BF16)
    same = (r0 >> 3) == (r1 >> 3)
    rank = within + dot(ones_where(same & (r1 < r0)), totals)
    count = dot(ones_where(same), totals)
    base = dot(ones_where((r1 >> 3) < (r0 >> 3)), totals)
    place = jnp.zeros((8, 128), F32)
    for j in range(OWNERS):
        at = slice(8 * j, 8 * j + 8)
        place += jnp.where(masks[j], rank[at] + base[at], 0.0)

    key = jnp.where(masks[0], rank[:8], -1.0)
    local_plus = (local + 1).astype(F32)
    slot_row = jnp.zeros((CAP, 128), F32)
    slots = iota((CAP, 128), 0).astype(F32)
    for r in range(8):
        slot_row += jnp.where(slots == key[r:r + 1], local_plus[r:r + 1], 0.0)
    cand_at = jnp.sum(slot_row, axis=1, keepdims=True)
    pick = pick_ref[...]
    pick_mine = jnp.broadcast_to((pick >> shift) == me, (8, 128))
    pick_rank = dot(ones_where(pick_mine), before)
    pick_key = jnp.where(pick_mine, pick_rank, -1.0)
    pick_plus = ((pick & (rows - 1)) + 1).astype(F32)
    pick_at = jnp.sum(
        jnp.where(iota((PCAP, 128), 0).astype(F32) == pick_key[:1], pick_plus, 0.0),
        axis=1, keepdims=True)
    at_row = jnp.concatenate([cand_at, pick_at], axis=0).astype(jnp.int32) - 1
    at_row = jnp.broadcast_to(at_row, (CAP + PCAP, chunk))

    lanes = iota((CAP + PCAP, chunk), 1)

    def gather(i, total):
        load(i).wait()
        at = pl.ds(pl.multiple_of(i * chunk, chunk), chunk)
        return total + dot(ones_where(at_row - i * chunk == lanes), emb[at, :])

    total = lax.fori_loop(0, chunks, gather, jnp.zeros((CAP + PCAP, emb.shape[1]), F32))
    pk[0] = total[CAP:].astype(BF16)
    blk[0] = total[:CAP].astype(BF16)

    pl.semaphore_wait(barrier, OWNERS - 1)

    def send(buf, src, dst, send_sem, recv_sem, rel):
        return pltpu.make_async_remote_copy(
            src_ref=buf.at[src], dst_ref=buf.at[dst], send_sem=send_sem, recv_sem=recv_sem.at[dst],
            device_id={"row": device(*rel)}, device_id_type=MESH)

    def send_own(buf, send_sems, recv_sems, rel):
        dz, dy, dc = rel
        return send(buf, 0, SLOT[dz, -dy % 4, dc], send_sems.at[SLOT[rel]], recv_sems, rel)

    def forward(j):
        dz, dy, _ = ORDER[j]
        return send(blk, j, SLOT[dz, dy, 1], blk_send.at[SLOT[dz, dy, 1]], blk_recv, (0, 0, 1))

    for rel in ORDER[1:]:
        send_own(pk, pk_send, pk_recv, rel).start()
    for rel in ORDER[1:]:
        if rel[2] == 0 or rel == (0, 0, 1):
            send_own(blk, blk_send, blk_recv, rel).start()

    def wait_block(j):
        dz, dy, dc = ORDER[j]
        send(blk, 0, j, blk_send.at[j], blk_recv, (0, 0, 1)).wait_recv()

    held = jnp.zeros((8, 128), F32)
    every = cand_ref[...] >> shift
    for o in range(OWNERS):
        hit = jnp.where(every == o, 1.0, 0.0).reshape(8, 8, 128).sum(axis=1)
        held = jnp.where(iota((8, 128), 1) == o, jnp.sum(hit, axis=1, keepdims=True), held)
    lane = iota((128, 128), 1)
    limits = [(hi, last, 1) for _, hi, _, last in TILES[:-1]] + [(lo, first, 0) for lo, _, first, _ in TILES[1:]]
    which = lane >> 4
    window = jnp.zeros((128, 128), jnp.int32)
    for k, (_, edge, _) in enumerate(limits):
        window = jnp.where(which == k, edge, window)
    prefix = ones_where((order_of(iota((128, 128), 0), lane & 15) < window) & (iota((128, 128), 0) < OWNERS))
    sums = dot(held.astype(BF16), prefix)
    bad = held > CAP
    for k, (bound, _, least) in enumerate(limits):
        off = sums < bound if least else sums > bound
        bad = bad | ((which[:8] == k) & off)
    pick_col = pick_col_ref[...] >> shift
    pick_hit = jnp.where(pick_col == iota((PICKS, 128), 1), 1.0, 0.0)
    pick_over = jnp.sum(pick_hit, axis=0, keepdims=True) > PCAP
    worst = jnp.maximum(jnp.max(jnp.where(bad, 1.0, 0.0)), jnp.max(jnp.where(pick_over, 1.0, 0.0)))
    flag_ref[0, 0] = worst.astype(jnp.int32)

    pick_order = order_of(pick_col, me)
    pick_one = ones_where(pick_order == iota((PICKS, 128), 1))
    earlier = dot(ones_where(iota((PICKS, PICKS), 1) < iota((PICKS, PICKS), 0)), pick_one)
    pick_rank_col = jnp.sum(jnp.where(pick_order == iota((PICKS, 128), 1), earlier, 0.0), axis=1, keepdims=True)
    pick_slot = pick_order[:, :1] * PCAP + pick_rank_col.astype(jnp.int32)
    for j in range(1, OWNERS):
        send(pk, 0, j, pk_send.at[j], pk_recv, (0, 0, 1)).wait_recv()
    picked = dot(
        ones_where(pick_slot == iota((PICKS, OWNERS * PCAP), 1)),
        pk[...].reshape(OWNERS * PCAP, emb.shape[1]))
    ch[:PICKS] = picked.astype(BF16)

    seen = {0}
    for t, (lo, hi, first, last) in enumerate(TILES):
        for j in range(last):
            if j not in seen and ORDER[j][2] == 0:
                wait_block(j)
                forward(j).start()
        for j in range(last):
            if j not in seen and ORDER[j][2] == 1:
                wait_block(j)
            seen.add(j)
        dense = jnp.zeros((hi - lo, emb.shape[1]), F32)
        for j in range(first, last):
            row = iota((hi - lo, CAP), 0) + lo
            slot = iota((hi - lo, CAP), 1)
            start = base[8 * j:8 * j + 1, :CAP].astype(jnp.int32)
            held_j = count[8 * j:8 * j + 1, :CAP].astype(jnp.int32)
            dense += dot(ones_where((row == start + slot) & (slot < held_j)), blk[j])
        ch[PICKS + lo:PICKS + hi] = dense.astype(BF16)
        acc[lo:hi] = jnp.zeros((hi - lo, 128), F32)

        def step(i, carry, t=t, lo=lo, hi=hi):
            e = emb[pl.ds(pl.multiple_of(i * block_rows, block_rows), block_rows), :]
            if t == 0:
                s = inner(ch[:PICKS + hi], e)
                cover = jnp.max(s[:PICKS], axis=0, keepdims=True)
                s = s[PICKS:]
            else:
                s = inner(ch[PICKS + lo:PICKS + hi], e)
            part = acc[lo:hi]
            for k in range(block_rows // 128):
                at = pl.ds(i * (block_rows // 128) + k, 1)
                lanes_k = slice(128 * k, 128 * k + 128)
                if t == 0:
                    cover_k = cover[:, lanes_k]
                    cover_ref[at, :] = cover_k
                else:
                    cover_k = cover_ref[at, :]
                part += jnp.maximum(s[:, lanes_k] - cover_k, 0.0)
            acc[lo:hi] = part
            return carry

        lax.fori_loop(0, rows // block_rows, step, 0)

    found = jnp.sum(acc[...], axis=1, keepdims=True)
    dense_at = iota((PER, 128), 0).astype(F32)
    parts = []
    for r in range(8):
        parts.append(jnp.sum(jnp.where(dense_at == place[r:r + 1], found, 0.0), axis=0, keepdims=True))
    red[me] = jnp.concatenate(parts, axis=0)

    def share(rel):
        return pltpu.make_async_remote_copy(
            src_ref=red.at[me], dst_ref=red.at[me], send_sem=red_send.at[SLOT[rel]], recv_sem=red_recv.at[me],
            device_id={"row": device(*rel)}, device_id_type=MESH)

    for rel in ORDER[1:]:
        share(rel).start()
    for rel in ORDER[1:]:
        o = device(*rel)
        pltpu.make_async_remote_copy(
            src_ref=red.at[me], dst_ref=red.at[o], send_sem=red_send.at[SLOT[rel]], recv_sem=red_recv.at[o],
            device_id={"row": o}, device_id_type=MESH).wait_recv()
    whole = red[0]
    for o in range(1, OWNERS):
        whole += red[o]
    gains_ref[...] = whole * (1.0 / (rows * OWNERS))

    for rel in ORDER[1:]:
        send_own(pk, pk_send, pk_recv, rel).wait_send()
        share(rel).wait_send()
        if rel[2] == 0 or rel == (0, 0, 1):
            send_own(blk, blk_send, blk_recv, rel).wait_send()
        if rel[2] == 0:
            forward(SLOT[rel]).wait_send()


def select_owned(embeddings, indices):
    count = embeddings.shape[0]
    local = indices - lax.axis_index("row") * count
    owned = (local >= 0) & (local < count)
    taken = jnp.take(embeddings, jnp.clip(local, 0, count - 1), axis=0)
    return jnp.where(owned[:, None], taken, jnp.zeros_like(taken))


def sum_over_rows(x):
    size = lax.axis_size("row")
    step = 1
    while step < size:
        x = x + lax.ppermute(x, "row", [(i, i ^ step) for i in range(size)])
        step *= 2
    return x


def whole_path(embeddings, pick_index, cand_index):
    count = embeddings.shape[0]
    per = cand_index.shape[0] // lax.axis_size("cand")
    mine = lax.dynamic_slice_in_dim(cand_index, lax.axis_index("cand") * per, per, 0)
    picked = sum_over_rows(select_owned(embeddings, pick_index))
    coverage = jnp.max(inner(embeddings, picked), axis=1)
    chosen = sum_over_rows(select_owned(embeddings, mine))
    similar = inner(embeddings, chosen)
    partial = jnp.sum(jnp.maximum(similar - coverage[:, None], 0.0), axis=0)
    return sum_over_rows(partial) / (count * lax.axis_size("row")), coverage


def per_device(embeddings, pick_index, cand_index):
    rows, width = embeddings.shape
    shift = rows.bit_length() - 1
    chunks = 8
    block_rows = 2048
    pick_row = jnp.concatenate([pick_index, jnp.full((128 - PICKS,), -1, jnp.int32)]).reshape(1, 128)
    vmem = pl.BlockSpec(memory_space=pltpu.VMEM)
    gains, cover, flag = pl.pallas_call(
        functools.partial(kernel, block_rows, shift),
        out_shape=[
            jax.ShapeDtypeStruct((8, 128), F32),
            jax.ShapeDtypeStruct((rows // 128, 128), F32),
            jax.ShapeDtypeStruct((1, 1), jnp.int32),
        ],
        in_specs=[vmem, vmem, vmem, pl.BlockSpec(memory_space=pl.ANY)],
        out_specs=[vmem, vmem, pl.BlockSpec(memory_space=pltpu.SMEM)],
        scratch_shapes=[
            pltpu.VMEM((rows, width), BF16),
            pltpu.VMEM((OWNERS, CAP, width), BF16),
            pltpu.VMEM((OWNERS, PCAP, width), BF16),
            pltpu.VMEM((PICKS + PER, width), BF16),
            pltpu.VMEM((PER, 128), F32),
            pltpu.VMEM((OWNERS, 8, 128), F32),
            pltpu.SemaphoreType.DMA((chunks,)),
            pltpu.SemaphoreType.DMA((OWNERS,)),
            pltpu.SemaphoreType.DMA((OWNERS,)),
            pltpu.SemaphoreType.DMA((OWNERS,)),
            pltpu.SemaphoreType.DMA((OWNERS,)),
            pltpu.SemaphoreType.DMA((OWNERS,)),
            pltpu.SemaphoreType.DMA((OWNERS,)),
        ],
        compiler_params=pltpu.CompilerParams(
            collective_id=0, has_side_effects=True, vmem_limit_bytes=60 * 2**20),
        cost_estimate=pl.CostEstimate(
            flops=2 * rows * (PER + PICKS) * width, bytes_accessed=2 * rows * width, transcendentals=0),
    )(cand_index.reshape(-1, 128), pick_row, pick_index.reshape(PICKS, 1), embeddings)
    return lax.cond(
        flag[0, 0] == 0,
        lambda: (gains.reshape(PER), cover.reshape(rows)),
        lambda: whole_path(embeddings, pick_index, cand_index),
    )


def solution(mesh):
    return jax.shard_map(
        per_device,
        mesh=mesh,
        in_specs=(P("row", None), P(), P()),
        out_specs=(P("cand"), P("row")),
        check_vma=False,
    )
```

```python
import functools

import jax
import jax.numpy as jnp
from jax import lax
from jax.experimental import pallas as pl
from jax.experimental.pallas import tpu as pltpu
from jax.sharding import PartitionSpec as P

MESH = pl.DeviceIdType.MESH
F32 = jnp.float32
BF16 = jnp.bfloat16

CHIPS = ((0, 0), (1, 0), (0, 1), (0, 3), (1, 1), (1, 3), (0, 2), (1, 2))
ORDER = tuple((dz, dy, dc) for dz, dy in CHIPS for dc in (0, 1))
SLOT = {rel: j for j, rel in enumerate(ORDER)}
OWNERS = 16
PER = 1024
PICKS = 64
PCAP = 16
UNIT = 48
REST = 272
PICK_AT = 2 * UNIT
REST_AT = OWNERS * UNIT + PICKS
STREAM = REST_AT + REST
PASSES = ((0, 96, 4096), (96, 448, 2048), (448, 640, 4096), (640, STREAM, 2048))


def unit_at(j):
    return UNIT * j + (PICKS if j >= 2 else 0)


def iota(shape, dim):
    return lax.broadcasted_iota(jnp.int32, shape, dim)


def dot(a, b):
    return jnp.dot(a, b, preferred_element_type=F32)


def inner(left, right):
    return lax.dot_general(left, right, (((1,), (1,)), ((), ())), preferred_element_type=F32)


def ones_where(cond):
    return jnp.where(cond, 1.0, 0.0).astype(BF16)


def order_of(owner, device):
    dz = (owner >> 3) ^ (device >> 3)
    dy = ((owner >> 1) - (device >> 1)) & 3
    chip = dz * 4 + dy
    place = jnp.zeros_like(chip)
    for rank, (cz, cy) in enumerate(CHIPS):
        place = jnp.where(chip == cz * 4 + cy, rank, place)
    return place * 2 + ((owner ^ device) & 1)


def kernel(
    shift,
    cand_hbm, pick_hbm, emb_hbm,
    gains_ref, cover_hbm, flag_ref,
    cand_ref, pick_ref, emb, ch, late, pk, raw, cover_ref, acc, red,
    in_sem, load_sem, pk_send, pk_recv, ch_send, ch_recv, late_send, late_recv, red_send, red_recv,
):
    rows = emb.shape[0]
    width = emb.shape[1]
    chunks = load_sem.shape[0]
    chunk = rows // chunks
    me = lax.axis_index("row")
    group = lax.axis_index("cand")
    z, y, c = me // 8, (me // 2) % 4, me % 2

    def device(dz, dy, dc):
        return (z + dz) % 2 * 8 + (y + dy) % 4 * 2 + (c + dc) % 2

    def load(i):
        at = pl.ds(pl.multiple_of(i * chunk, chunk), chunk)
        return pltpu.make_async_copy(emb_hbm.at[at], emb.at[at], load_sem.at[i])

    cand_in = pltpu.make_async_copy(cand_hbm, cand_ref, in_sem.at[0])
    pick_in = pltpu.make_async_copy(pick_hbm, pick_ref, in_sem.at[1])
    cover_out = pltpu.make_async_copy(cover_ref, cover_hbm, in_sem.at[2])
    cand_in.start()
    pick_in.start()
    for i in range(chunks):
        load(i).start()

    barrier = pltpu.get_barrier_semaphore()
    for rel in ORDER[1:]:
        pl.semaphore_signal(barrier, inc=1, device_id={"row": device(*rel)}, device_id_type=MESH)
    cand_in.wait()
    pick_in.wait()

    mine = cand_ref[pl.ds(pl.multiple_of(group * 8, 8), 8), :]
    owner, local = mine >> shift, mine & (rows - 1)
    masks = [owner == device(*rel) for rel in ORDER]
    mask = jnp.concatenate([jnp.where(m, 1.0, 0.0) for m in masks], axis=0).astype(BF16)
    r0, r1 = iota((128, 128), 0), iota((128, 128), 1)
    before = ones_where(r0 < r1)
    within = dot(mask, before)
    totals = dot(mask, jnp.ones((128, 128), BF16)).astype(BF16)
    same = (r0 >> 3) == (r1 >> 3)
    rank = within + dot(ones_where(same & (r1 < r0)), totals)

    slots = iota((2 * UNIT, 128), 0).astype(F32)
    key = jnp.where(masks[0], rank[:8], -1.0)
    local_plus = (local + 1).astype(F32)
    slot_row = jnp.zeros((2 * UNIT, 128), F32)
    for r in range(8):
        slot_row += jnp.where(slots == key[r:r + 1], local_plus[r:r + 1], 0.0)
    cand_at = jnp.sum(slot_row, axis=1, keepdims=True)
    pick = pick_ref[...]
    pick_mine = (pick >> shift) == me
    pick_rank = dot(ones_where(jnp.broadcast_to(pick_mine, (8, PICKS))), before[:PICKS, :PICKS])
    pick_key = jnp.where(pick_mine, pick_rank[:1], -1.0)
    pick_plus = ((pick & (rows - 1)) + 1).astype(F32)
    pick_at = jnp.sum(
        jnp.where(iota((PCAP, PICKS), 0).astype(F32) == pick_key, pick_plus, 0.0), axis=1, keepdims=True)
    held_rows = 2 * UNIT + PCAP
    at_row = jnp.concatenate([cand_at, pick_at], axis=0).astype(jnp.int32) - 1
    at_row = jnp.broadcast_to(at_row, (held_rows, chunk))

    lanes = iota((held_rows, chunk), 1)

    def gather(i, total):
        load(i).wait()
        at = pl.ds(pl.multiple_of(i * chunk, chunk), chunk)
        return total + dot(ones_where(at_row - i * chunk == lanes), emb[at, :])

    total = lax.fori_loop(0, chunks, gather, jnp.zeros((held_rows, width), F32))
    pk[0] = total[2 * UNIT:].astype(BF16)
    ch[:UNIT] = total[:UNIT].astype(BF16)
    late[0] = total[UNIT:2 * UNIT].astype(BF16)

    pl.semaphore_wait(barrier, OWNERS - 1)

    def remote(src, dst, send_sem, recv_sem, to):
        return pltpu.make_async_remote_copy(
            src_ref=src, dst_ref=dst, send_sem=send_sem, recv_sem=recv_sem,
            device_id={"row": to}, device_id_type=MESH)

    def ch_block(j):
        return ch.at[pl.ds(unit_at(j), UNIT)]

    def late_block(j):
        return late.at[j]

    def pk_block(j):
        return pk.at[j]

    CH = (ch_block, ch_send, ch_recv)
    LATE = (late_block, late_send, late_recv)
    PK = (pk_block, pk_send, pk_recv)

    def own(part, rel):
        block, sent, got = part
        dz, dy, dc = rel
        to = SLOT[dz, -dy % 4, dc]
        return remote(block(0), block(to), sent.at[SLOT[rel]], got.at[to], device(*rel))

    def hand(part, chip):
        block, sent, got = part
        j = SLOT[(*chip, 0)]
        return remote(block(j), block(j + 1), sent.at[j + 1], got.at[j + 1], device(0, 0, 1))

    def relay(part, dz):
        block, sent, got = part
        to = SLOT[dz, 2, 0]
        first = SLOT[dz, 3, 0] - 2 * c
        if part is CH:
            src = ch.at[pl.ds(pl.multiple_of(first * UNIT + PICKS, 16), UNIT)]
        else:
            src = block(first)
        return remote(src, block(to), sent.at[to], got.at[to], device(0, 1 + 2 * c, 0))

    def arrived(part, *js):
        block, sent, got = part
        for j in js:
            remote(block(0), block(j), sent.at[j], got.at[j], device(0, 0, 1)).wait_recv()

    SIB = (0, 0, 1)
    NEAR = ((1, 0), (0, 1), (0, 3))
    DIAG = ((1, 1), (1, 3))
    FAR = ((0, 2), (1, 2))

    def evens(chips):
        return [SLOT[(*chip, 0)] for chip in chips]

    def odds(chips):
        return [SLOT[(*chip, 1)] for chip in chips]

    own(PK, SIB).start()
    for chip in FAR + DIAG + NEAR:
        own(PK, (*chip, 0)).start()
    own(CH, SIB).start()
    for chip in NEAR + DIAG:
        own(CH, (*chip, 0)).start()

    held = jnp.zeros((8, 128), F32)
    every = cand_ref[...] >> shift
    lane8 = iota((8, 128), 1)
    for o in range(OWNERS):
        hit = jnp.where(every == o, 1.0, 0.0).reshape(8, 8, 128).sum(axis=1)
        held = jnp.where(lane8 == o, jnp.sum(hit, axis=1, keepdims=True), held)
    over = jnp.maximum(held - UNIT, 0.0)
    bad = (over > UNIT) | (jnp.sum(over, axis=1, keepdims=True) > REST)
    eye = iota((PICKS, PICKS), 0) == iota((PICKS, PICKS), 1)
    pick_col = jnp.sum(jnp.where(eye, (pick >> shift).astype(F32), 0.0), axis=1, keepdims=True).astype(jnp.int32)
    pick_hit = jnp.where(pick_col == iota((PICKS, 128), 1), 1.0, 0.0)
    pick_over = jnp.sum(pick_hit, axis=0, keepdims=True) > PCAP
    worst = jnp.maximum(jnp.max(jnp.where(bad, 1.0, 0.0)), jnp.max(jnp.where(pick_over, 1.0, 0.0)))
    flag_ref[0, 0] = worst.astype(jnp.int32)

    count = dot(ones_where(same), totals)
    rest = jnp.maximum(count - UNIT, 0.0).astype(BF16)
    rest_base = dot(ones_where(((r1 >> 3) < (r0 >> 3)) & ((r1 & 7) == 0)), rest)
    place = jnp.zeros((8, 128), F32)
    for j in range(OWNERS):
        at = slice(8 * j, 8 * j + 8)
        row = jnp.where(rank[at] < UNIT, rank[at] + unit_at(j), rank[at] + (rest_base[at] + (REST_AT - UNIT)))
        place += jnp.where(masks[j], row, 0.0)

    pick_order = order_of(pick_col, me)
    pick_one = ones_where(pick_order == iota((PICKS, 128), 1))
    earlier = dot(ones_where(iota((PICKS, PICKS), 1) < iota((PICKS, PICKS), 0)), pick_one)
    pick_rank_col = jnp.sum(jnp.where(pick_order == iota((PICKS, 128), 1), earlier, 0.0), axis=1, keepdims=True)
    pick_slot = pick_order * PCAP + pick_rank_col.astype(jnp.int32)
    pick_pack = ones_where(pick_slot == iota((PICKS, OWNERS * PCAP), 1))
    group_over = jnp.where(iota((8, 128), 0) == group, over, 0.0).astype(BF16)
    late_slots = OWNERS * UNIT
    block_of = (iota((128, late_slots), 1) * 1366) >> 16
    order_col = order_of(iota((128, late_slots), 0), me)
    order_col = jnp.where(iota((128, late_slots), 0) < OWNERS, order_col, OWNERS)
    late_base = jnp.sum(dot(group_over, ones_where(order_col < block_of)), axis=0, keepdims=True)
    late_count = jnp.sum(dot(group_over, ones_where(order_col == block_of)), axis=0, keepdims=True)
    late_slot = (iota((1, late_slots), 1) - block_of[:1] * UNIT).astype(F32)
    late_row = jnp.where(late_slot < late_count, late_base + late_slot, -1.0)

    def one_pass(t, polls):
        lo, hi, step_rows = PASSES[t]
        acc[lo:hi] = jnp.zeros((hi - lo, 128), F32)
        groups = step_rows // 128

        def step(i, carry):
            e = emb[pl.ds(pl.multiple_of(i * step_rows, step_rows), step_rows), :]
            s = inner(ch[lo:hi], e)
            if t == 0:
                raw[:, pl.ds(pl.multiple_of(i * step_rows, step_rows), step_rows)] = s
            else:
                if t == 1:
                    cover = jnp.max(s[:PICKS], axis=0, keepdims=True)
                    s = s[PICKS:]
                    held_back = acc[:PICK_AT]
                at_acc = lo + PICKS if t == 1 else lo
                part = acc[at_acc:hi]
                for k in range(groups):
                    at = pl.ds(i * groups + k, 1)
                    lanes_k = slice(128 * k, 128 * k + 128)
                    if t == 1:
                        cover_k = cover[:, lanes_k]
                        cover_ref[at, :] = cover_k
                        raw_k = raw[:, pl.ds(pl.multiple_of(i * step_rows + 128 * k, 128), 128)]
                        held_back += jnp.maximum(raw_k - cover_k, 0.0)
                    else:
                        cover_k = cover_ref[at, :]
                    part += jnp.maximum(s[:, lanes_k] - cover_k, 0.0)
                acc[at_acc:hi] = part
                if t == 1:
                    acc[:PICK_AT] = held_back
            for n, poll in polls.items():
                pl.when(i == n)(poll)
            return carry

        lax.fori_loop(0, rows // step_rows, step, 0)

    def hand_all(part, chips):
        arrived(part, *evens(chips))
        for chip in chips:
            hand(part, chip).start()

    def near(part):
        hand_all(part, NEAR)
        relay(part, 0).start()

    def diagonal(part):
        hand_all(part, DIAG)
        relay(part, 1).start()

    def far(part):
        hand_all(part, FAR)

    def send_late():
        own(LATE, SIB).start()
        for chip in NEAR + DIAG:
            own(LATE, (*chip, 0)).start()

    arrived(CH, SLOT[SIB])
    one_pass(0, {0: lambda: hand_all(PK, NEAR)})
    hand_all(PK, DIAG)
    near(CH)
    hand_all(PK, FAR)
    arrived(PK, *range(1, OWNERS, 2))
    send_late()
    ch[PICK_AT:PICK_AT + PICKS] = dot(pick_pack, pk[...].reshape(OWNERS * PCAP, width)).astype(BF16)
    arrived(CH, *odds(NEAR))
    acc[:PICK_AT] = jnp.zeros((PICK_AT, 128), F32)
    one_pass(1, {0: lambda: diagonal(CH), 1: lambda: far(CH), 2: lambda: near(LATE)})
    cover_out.start()
    arrived(CH, *odds(DIAG))
    one_pass(2, {0: lambda: diagonal(LATE)})
    far(LATE)
    arrived(CH, *odds(FAR))
    arrived(LATE, *range(1, OWNERS, 2))
    packed = dot(ones_where(iota((REST, late_slots), 0).astype(F32) == late_row), late[...].reshape(late_slots, width))
    ch[REST_AT:] = packed.astype(BF16)
    one_pass(3, {})

    found = jnp.sum(acc[...], axis=1, keepdims=True)
    dense_at = iota((STREAM, 128), 0).astype(F32)
    parts = []
    for r in range(8):
        parts.append(jnp.sum(jnp.where(dense_at == place[r:r + 1], found, 0.0), axis=0, keepdims=True))
    red[me] = jnp.concatenate(parts, axis=0)

    def share(rel, at):
        return remote(red.at[me], red.at[at], red_send.at[SLOT[rel]], red_recv.at[at], device(*rel))

    for rel in ORDER[:0:-1]:
        share(rel, me).start()
    for rel in ORDER[1:]:
        share(rel, device(*rel)).wait_recv()
    whole = red[0]
    for o in range(1, OWNERS):
        whole += red[o]
    gains_ref[...] = whole * (1.0 / (rows * OWNERS))

    cover_out.wait()
    for rel in ORDER[1:]:
        share(rel, me).wait_send()
    for part in (PK, CH, LATE):
        own(part, SIB).wait_send()
        for chip in NEAR + DIAG:
            own(part, (*chip, 0)).wait_send()
            hand(part, chip).wait_send()
        for chip in FAR:
            if part is PK:
                own(part, (*chip, 0)).wait_send()
            else:
                relay(part, chip[0]).wait_send()
            hand(part, chip).wait_send()


def select_owned(embeddings, indices):
    count = embeddings.shape[0]
    local = indices - lax.axis_index("row") * count
    owned = (local >= 0) & (local < count)
    taken = jnp.take(embeddings, jnp.clip(local, 0, count - 1), axis=0)
    return jnp.where(owned[:, None], taken, jnp.zeros_like(taken))


def sum_over_rows(x):
    size = lax.axis_size("row")
    step = 1
    while step < size:
        x = x + lax.ppermute(x, "row", [(i, i ^ step) for i in range(size)])
        step *= 2
    return x


def whole_path(embeddings, pick_index, cand_index):
    count = embeddings.shape[0]
    per = cand_index.shape[0] // lax.axis_size("cand")
    mine = lax.dynamic_slice_in_dim(cand_index, lax.axis_index("cand") * per, per, 0)
    picked = sum_over_rows(select_owned(embeddings, pick_index))
    coverage = jnp.max(inner(embeddings, picked), axis=1)
    chosen = sum_over_rows(select_owned(embeddings, mine))
    similar = inner(embeddings, chosen)
    partial = jnp.sum(jnp.maximum(similar - coverage[:, None], 0.0), axis=0)
    return sum_over_rows(partial) / (count * lax.axis_size("row")), coverage


def per_device(embeddings, pick_index, cand_index):
    rows, width = embeddings.shape
    shift = rows.bit_length() - 1
    chunks = 8
    anywhere = pl.BlockSpec(memory_space=pl.ANY)
    dma = pltpu.SemaphoreType.DMA
    gains, cover, flag = pl.pallas_call(
        functools.partial(kernel, shift),
        out_shape=[
            jax.ShapeDtypeStruct((8, 128), F32),
            jax.ShapeDtypeStruct((rows // 128, 128), F32),
            jax.ShapeDtypeStruct((1, 1), jnp.int32),
        ],
        in_specs=[anywhere, anywhere, anywhere],
        out_specs=[pl.BlockSpec(memory_space=pltpu.VMEM), anywhere, pl.BlockSpec(memory_space=pltpu.SMEM)],
        scratch_shapes=[
            pltpu.VMEM((64, 128), jnp.int32),
            pltpu.VMEM((1, PICKS), jnp.int32),
            pltpu.VMEM((rows, width), BF16),
            pltpu.VMEM((STREAM, width), BF16),
            pltpu.VMEM((OWNERS, UNIT, width), BF16),
            pltpu.VMEM((OWNERS, PCAP, width), BF16),
            pltpu.VMEM((2 * UNIT, rows), F32),
            pltpu.VMEM((rows // 128, 128), F32),
            pltpu.VMEM((STREAM, 128), F32),
            pltpu.VMEM((OWNERS, 8, 128), F32),
            dma((3,)), dma((chunks,)),
        ] + [dma((OWNERS,))] * 8,
        compiler_params=pltpu.CompilerParams(
            collective_id=0, has_side_effects=True, vmem_limit_bytes=60 * 2**20),
        cost_estimate=pl.CostEstimate(
            flops=2 * rows * (PER + PICKS) * width, bytes_accessed=2 * rows * width, transcendentals=0),
    )(cand_index.reshape(-1, 128), pick_index.reshape(1, PICKS), embeddings)
    return lax.cond(
        flag[0, 0] == 0,
        lambda: (gains.reshape(PER), cover.reshape(rows)),
        lambda: whole_path(embeddings, pick_index, cand_index),
    )


def solution(mesh):
    return jax.shard_map(
        per_device,
        mesh=mesh,
        in_specs=(P("row", None), P(), P()),
        out_specs=(P("cand"), P("row")),
        check_vma=False,
    )
```

```python
import functools

import jax
import jax.numpy as jnp
from jax import lax
from jax.experimental import pallas as pl
from jax.experimental.pallas import tpu as pltpu
from jax.sharding import PartitionSpec as P

MESH = pl.DeviceIdType.MESH
F32 = jnp.float32
BF16 = jnp.bfloat16

CHIPS = ((0, 0), (1, 0), (0, 1), (0, 3), (1, 1), (1, 3), (0, 2), (1, 2))
ORDER = tuple((dz, dy, dc) for dz, dy in CHIPS for dc in (0, 1))
SLOT = {rel: j for j, rel in enumerate(ORDER)}
OWNERS = 16
PER = 1024
PICKS = 64
PCAP = 16
UNIT = 48
REST = 272
PICK_AT = 2 * UNIT
REST_AT = OWNERS * UNIT + PICKS
STREAM = REST_AT + REST
PASSES = ((0, PICK_AT), (PICK_AT, 448), (448, 736), (736, STREAM))
STEP_ROWS = 2048


def unit_at(j):
    return UNIT * j + (PICKS if j >= 2 else 0)


def iota(shape, dim):
    return lax.broadcasted_iota(jnp.int32, shape, dim)


def dot(a, b):
    return jnp.dot(a, b, preferred_element_type=F32)


def inner(left, right):
    return lax.dot_general(left, right, (((1,), (1,)), ((), ())), preferred_element_type=F32)


def ones_where(cond):
    return jnp.where(cond, 1.0, 0.0).astype(BF16)


def order_of(owner, device):
    dz = (owner >> 3) ^ (device >> 3)
    dy = ((owner >> 1) - (device >> 1)) & 3
    chip = dz * 4 + dy
    place = jnp.zeros_like(chip)
    for rank, (cz, cy) in enumerate(CHIPS):
        place = jnp.where(chip == cz * 4 + cy, rank, place)
    return place * 2 + ((owner ^ device) & 1)


def kernel(
    shift,
    cand_hbm, pick_hbm, emb_hbm,
    gains_ref, cover_hbm, flag_ref,
    cand_ref, pick_ref, emb, ch, late, pk, raw, cover_ref, acc, red,
    in_sem, load_sem, pk_send, pk_recv, ch_send, ch_recv, late_send, late_recv, red_send, red_recv,
):
    rows = emb.shape[0]
    width = emb.shape[1]
    chunks = load_sem.shape[0]
    chunk = rows // chunks
    me = lax.axis_index("row")
    group = lax.axis_index("cand")
    z, y, c = me // 8, (me // 2) % 4, me % 2

    def device(dz, dy, dc):
        return (z + dz) % 2 * 8 + (y + dy) % 4 * 2 + (c + dc) % 2

    def load(i):
        at = pl.ds(pl.multiple_of(i * chunk, chunk), chunk)
        return pltpu.make_async_copy(emb_hbm.at[at], emb.at[at], load_sem.at[i])

    cand_in = pltpu.make_async_copy(cand_hbm, cand_ref, in_sem.at[0])
    pick_in = pltpu.make_async_copy(pick_hbm, pick_ref, in_sem.at[1])
    cover_out = pltpu.make_async_copy(cover_ref, cover_hbm, in_sem.at[2])
    cand_in.start()
    pick_in.start()
    for i in range(chunks):
        load(i).start()

    barrier = pltpu.get_barrier_semaphore()
    for rel in ORDER[1:]:
        pl.semaphore_signal(barrier, inc=1, device_id={"row": device(*rel)}, device_id_type=MESH)
    cand_in.wait()
    pick_in.wait()

    mine = cand_ref[pl.ds(pl.multiple_of(group * 8, 8), 8), :]
    owner, local = mine >> shift, mine & (rows - 1)
    masks = [owner == device(*rel) for rel in ORDER]
    mask = jnp.concatenate([jnp.where(m, 1.0, 0.0) for m in masks], axis=0).astype(BF16)
    r0, r1 = iota((128, 128), 0), iota((128, 128), 1)
    before = ones_where(r0 < r1)
    within = dot(mask, before)
    totals = dot(mask, jnp.ones((128, 128), BF16)).astype(BF16)
    same = (r0 >> 3) == (r1 >> 3)
    rank = within + dot(ones_where(same & (r1 < r0)), totals)

    slots = iota((2 * UNIT, 128), 0).astype(F32)
    key = jnp.where(masks[0], rank[:8], -1.0)
    local_plus = (local + 1).astype(F32)
    slot_row = jnp.zeros((2 * UNIT, 128), F32)
    for r in range(8):
        slot_row += jnp.where(slots == key[r:r + 1], local_plus[r:r + 1], 0.0)
    cand_at = jnp.sum(slot_row, axis=1, keepdims=True)
    pick = pick_ref[...]
    pick_mine = (pick >> shift) == me
    pick_rank = dot(ones_where(jnp.broadcast_to(pick_mine, (8, PICKS))), before[:PICKS, :PICKS])
    pick_key = jnp.where(pick_mine, pick_rank[:1], -1.0)
    pick_plus = ((pick & (rows - 1)) + 1).astype(F32)
    pick_at = jnp.sum(
        jnp.where(iota((PCAP, PICKS), 0).astype(F32) == pick_key, pick_plus, 0.0), axis=1, keepdims=True)
    held_rows = 2 * UNIT + PCAP
    at_row = jnp.concatenate([cand_at, pick_at], axis=0).astype(jnp.int32) - 1
    at_row = jnp.broadcast_to(at_row, (held_rows, chunk))

    lanes = iota((held_rows, chunk), 1)

    def gather(i, total):
        load(i).wait()
        at = pl.ds(pl.multiple_of(i * chunk, chunk), chunk)
        return total + dot(ones_where(at_row - i * chunk == lanes), emb[at, :])

    total = lax.fori_loop(0, chunks, gather, jnp.zeros((held_rows, width), F32))
    pk[0] = total[2 * UNIT:].astype(BF16)
    ch[:UNIT] = total[:UNIT].astype(BF16)
    late[0] = total[UNIT:2 * UNIT].astype(BF16)

    pl.semaphore_wait(barrier, OWNERS - 1)

    def remote(src, dst, send_sem, recv_sem, to):
        return pltpu.make_async_remote_copy(
            src_ref=src, dst_ref=dst, send_sem=send_sem, recv_sem=recv_sem,
            device_id={"row": to}, device_id_type=MESH)

    def ch_block(j):
        return ch.at[pl.ds(unit_at(j), UNIT)]

    def late_block(j):
        return late.at[j]

    def pk_block(j):
        return pk.at[j]

    CH = (ch_block, ch_send, ch_recv)
    LATE = (late_block, late_send, late_recv)
    PK = (pk_block, pk_send, pk_recv)

    def own(part, rel):
        block, sent, got = part
        dz, dy, dc = rel
        to = SLOT[dz, -dy % 4, dc]
        return remote(block(0), block(to), sent.at[SLOT[rel]], got.at[to], device(*rel))

    def hand(part, chip):
        block, sent, got = part
        j = SLOT[(*chip, 0)]
        return remote(block(j), block(j + 1), sent.at[j + 1], got.at[j + 1], device(0, 0, 1))

    def moved(part, src, to, device_to):
        block, sent, got = part
        if part is CH:
            ref = ch.at[pl.ds(pl.multiple_of(src * UNIT + PICKS, 16), UNIT)]
        else:
            ref = block(src)
        return remote(ref, block(to), sent.at[to], got.at[to], device_to)

    def relay(part, dz):
        return moved(part, SLOT[dz, 3, 0] - 2 * c, SLOT[dz, 2, 0], device(0, 1 + 2 * c, 0))

    def across(part, dy):
        along_y = SLOT[0, dy, 0]
        src = along_y - c * (along_y - SLOT[1, 0, 0])
        return moved(part, src, SLOT[1, dy, 0], device(1 - c, c * (-dy % 4), 0))

    def arrived(part, *js):
        block, sent, got = part
        for j in js:
            remote(block(0), block(j), sent.at[j], got.at[j], device(0, 0, 1)).wait_recv()

    SIB = (0, 0, 1)
    NEAR = ((1, 0), (0, 1), (0, 3))
    DIAG = ((1, 1), (1, 3))
    FAR = ((0, 2), (1, 2))

    def evens(chips):
        return [SLOT[(*chip, 0)] for chip in chips]

    def odds(chips):
        return [SLOT[(*chip, 1)] for chip in chips]

    for chip in NEAR:
        own(CH, (*chip, 0)).start()
    own(CH, SIB).start()
    for chip in FAR + DIAG + NEAR:
        own(PK, (*chip, 0)).start()
    own(PK, SIB).start()

    held = jnp.zeros((8, 128), F32)
    every = cand_ref[...] >> shift
    lane8 = iota((8, 128), 1)
    for o in range(OWNERS):
        hit = jnp.where(every == o, 1.0, 0.0).reshape(8, 8, 128).sum(axis=1)
        held = jnp.where(lane8 == o, jnp.sum(hit, axis=1, keepdims=True), held)
    over = jnp.maximum(held - UNIT, 0.0)
    bad = (over > UNIT) | (jnp.sum(over, axis=1, keepdims=True) > REST)
    eye = iota((PICKS, PICKS), 0) == iota((PICKS, PICKS), 1)
    pick_col = jnp.sum(jnp.where(eye, (pick >> shift).astype(F32), 0.0), axis=1, keepdims=True).astype(jnp.int32)
    pick_hit = jnp.where(pick_col == iota((PICKS, 128), 1), 1.0, 0.0)
    pick_over = jnp.sum(pick_hit, axis=0, keepdims=True) > PCAP
    worst = jnp.maximum(jnp.max(jnp.where(bad, 1.0, 0.0)), jnp.max(jnp.where(pick_over, 1.0, 0.0)))
    flag_ref[0, 0] = worst.astype(jnp.int32)

    count = dot(ones_where(same), totals)
    rest = jnp.maximum(count - UNIT, 0.0).astype(BF16)
    rest_base = dot(ones_where(((r1 >> 3) < (r0 >> 3)) & ((r1 & 7) == 0)), rest)
    place = jnp.zeros((8, 128), F32)
    for j in range(OWNERS):
        at = slice(8 * j, 8 * j + 8)
        row = jnp.where(rank[at] < UNIT, rank[at] + unit_at(j), rank[at] + (rest_base[at] + (REST_AT - UNIT)))
        place += jnp.where(masks[j], row, 0.0)

    pick_order = order_of(pick_col, me)
    pick_one = ones_where(pick_order == iota((PICKS, 128), 1))
    earlier = dot(ones_where(iota((PICKS, PICKS), 1) < iota((PICKS, PICKS), 0)), pick_one)
    pick_rank_col = jnp.sum(jnp.where(pick_order == iota((PICKS, 128), 1), earlier, 0.0), axis=1, keepdims=True)
    pick_slot = pick_order * PCAP + pick_rank_col.astype(jnp.int32)
    pick_pack = ones_where(pick_slot == iota((PICKS, OWNERS * PCAP), 1))
    group_over = jnp.where(iota((8, 128), 0) == group, over, 0.0).astype(BF16)
    late_slots = OWNERS * UNIT
    block_of = (iota((128, late_slots), 1) * 1366) >> 16
    order_col = order_of(iota((128, late_slots), 0), me)
    order_col = jnp.where(iota((128, late_slots), 0) < OWNERS, order_col, OWNERS)
    late_base = jnp.sum(dot(group_over, ones_where(order_col < block_of)), axis=0, keepdims=True)
    late_count = jnp.sum(dot(group_over, ones_where(order_col == block_of)), axis=0, keepdims=True)
    late_slot = (iota((1, late_slots), 1) - block_of[:1] * UNIT).astype(F32)
    late_row = jnp.where(late_slot < late_count, late_base + late_slot, -1.0)

    def gain_of(get, covers, lo, hi):
        for top in range(lo, hi, 64):
            end = min(top + 64, hi)
            part = acc[top:end]
            for k, cover in enumerate(covers):
                part += jnp.maximum(get(top, end, k) - cover, 0.0)
            acc[top:end] = part

    def one_pass(t, polls):
        lo, hi = PASSES[t]
        groups = STEP_ROWS // 128

        def step(i, carry):
            at = pl.multiple_of(i * STEP_ROWS, STEP_ROWS)
            s = inner(ch[lo:hi], emb[pl.ds(at, STEP_ROWS), :])

            def kept(top, end, k):
                return raw[top:end, pl.ds(pl.multiple_of(at + 128 * k, 128), 128)]

            def new(top, end, k):
                return s[top - lo:end - lo, 128 * k:128 * k + 128]

            if t == 0:
                raw[:, pl.ds(at, STEP_ROWS)] = s
            elif t == 1:
                cover = jnp.max(s[:PICKS], axis=0, keepdims=True)
                covers = [cover[:, 128 * k:128 * k + 128] for k in range(groups)]
                for k in range(groups):
                    cover_ref[pl.ds(i * groups + k, 1), :] = covers[k]
                gain_of(kept, covers, 0, PICK_AT)
                gain_of(new, covers, PICK_AT + PICKS, hi)
            else:
                covers = [cover_ref[pl.ds(i * groups + k, 1), :] for k in range(groups)]
                gain_of(new, covers, lo, hi)
            for n, todo in polls.items():
                @pl.when(i == n)
                def _(todo=todo):
                    for act in todo:
                        act()
            return carry

        lax.fori_loop(0, rows // STEP_ROWS, step, 0)

    def hand_all(part, chips):
        arrived(part, *evens(chips))
        for chip in chips:
            hand(part, chip).start()

    def near(part):
        arrived(part, *evens(NEAR))
        for dy in (1, 3):
            across(part, dy).start()
        relay(part, 0).start()
        for chip in NEAR:
            hand(part, chip).start()

    def diagonal(part):
        arrived(part, *evens(DIAG))
        relay(part, 1).start()
        for chip in DIAG:
            hand(part, chip).start()

    def send_late():
        for chip in NEAR:
            own(LATE, (*chip, 0)).start()
        own(LATE, SIB).start()

    acc[...] = jnp.zeros((STREAM, 128), F32)
    arrived(CH, SLOT[SIB])
    one_pass(0, {2: [lambda: near(CH), send_late, lambda: hand_all(PK, NEAR + DIAG)]})
    hand_all(PK, FAR)
    arrived(CH, *odds(NEAR))
    arrived(PK, *range(1, OWNERS, 2))
    ch[PICK_AT:PICK_AT + PICKS] = dot(pick_pack, pk[...].reshape(OWNERS * PCAP, width)).astype(BF16)
    one_pass(1, {
        0: [lambda: diagonal(CH)],
        1: [lambda: near(LATE), lambda: hand_all(CH, FAR[:1])],
        3: [lambda: hand_all(CH, FAR[1:]), lambda: diagonal(LATE)],
    })
    cover_out.start()
    arrived(CH, *odds(DIAG + FAR[:1]))
    one_pass(2, {
        0: [lambda: hand_all(LATE, FAR[:1])],
        2: [lambda: hand_all(LATE, FAR[1:])],
    })
    arrived(CH, *odds(FAR[1:]))
    arrived(LATE, *range(1, OWNERS, 2))
    packed = dot(ones_where(iota((REST, late_slots), 0).astype(F32) == late_row), late[...].reshape(late_slots, width))
    ch[REST_AT:] = packed.astype(BF16)
    one_pass(3, {})

    found = jnp.sum(acc[...], axis=1, keepdims=True)
    dense_at = iota((STREAM, 128), 0).astype(F32)
    parts = []
    for r in range(8):
        parts.append(jnp.sum(jnp.where(dense_at == place[r:r + 1], found, 0.0), axis=0, keepdims=True))
    red[me] = jnp.concatenate(parts, axis=0)

    def share(rel, at):
        return remote(red.at[me], red.at[at], red_send.at[SLOT[rel]], red_recv.at[at], device(*rel))

    for rel in ORDER[:0:-1]:
        share(rel, me).start()
    for rel in ORDER[1:]:
        share(rel, device(*rel)).wait_recv()
    whole = red[0]
    for o in range(1, OWNERS):
        whole += red[o]
    gains_ref[...] = whole * (1.0 / (rows * OWNERS))

    cover_out.wait()
    for rel in ORDER[1:]:
        share(rel, me).wait_send()
    for part in (PK, CH, LATE):
        own(part, SIB).wait_send()
        for chip in NEAR + DIAG + FAR:
            if part is PK or chip in NEAR:
                own(part, (*chip, 0)).wait_send()
            elif chip in DIAG:
                across(part, chip[1]).wait_send()
            else:
                relay(part, chip[0]).wait_send()
            hand(part, chip).wait_send()


def select_owned(embeddings, indices):
    count = embeddings.shape[0]
    local = indices - lax.axis_index("row") * count
    owned = (local >= 0) & (local < count)
    taken = jnp.take(embeddings, jnp.clip(local, 0, count - 1), axis=0)
    return jnp.where(owned[:, None], taken, jnp.zeros_like(taken))


def sum_over_rows(x):
    size = lax.axis_size("row")
    step = 1
    while step < size:
        x = x + lax.ppermute(x, "row", [(i, i ^ step) for i in range(size)])
        step *= 2
    return x


def whole_path(embeddings, pick_index, cand_index):
    count = embeddings.shape[0]
    per = cand_index.shape[0] // lax.axis_size("cand")
    mine = lax.dynamic_slice_in_dim(cand_index, lax.axis_index("cand") * per, per, 0)
    picked = sum_over_rows(select_owned(embeddings, pick_index))
    coverage = jnp.max(inner(embeddings, picked), axis=1)
    chosen = sum_over_rows(select_owned(embeddings, mine))
    similar = inner(embeddings, chosen)
    partial = jnp.sum(jnp.maximum(similar - coverage[:, None], 0.0), axis=0)
    return sum_over_rows(partial) / (count * lax.axis_size("row")), coverage


def per_device(embeddings, pick_index, cand_index):
    rows, width = embeddings.shape
    shift = rows.bit_length() - 1
    chunks = 4
    anywhere = pl.BlockSpec(memory_space=pl.ANY)
    dma = pltpu.SemaphoreType.DMA
    gains, cover, flag = pl.pallas_call(
        functools.partial(kernel, shift),
        out_shape=[
            jax.ShapeDtypeStruct((8, 128), F32),
            jax.ShapeDtypeStruct((rows // 128, 128), F32),
            jax.ShapeDtypeStruct((1, 1), jnp.int32),
        ],
        in_specs=[anywhere, anywhere, anywhere],
        out_specs=[pl.BlockSpec(memory_space=pltpu.VMEM), anywhere, pl.BlockSpec(memory_space=pltpu.SMEM)],
        scratch_shapes=[
            pltpu.VMEM((64, 128), jnp.int32),
            pltpu.VMEM((1, PICKS), jnp.int32),
            pltpu.VMEM((rows, width), BF16),
            pltpu.VMEM((STREAM, width), BF16),
            pltpu.VMEM((OWNERS, UNIT, width), BF16),
            pltpu.VMEM((OWNERS, PCAP, width), BF16),
            pltpu.VMEM((PICK_AT, rows), F32),
            pltpu.VMEM((rows // 128, 128), F32),
            pltpu.VMEM((STREAM, 128), F32),
            pltpu.VMEM((OWNERS, 8, 128), F32),
            dma((3,)), dma((chunks,)),
        ] + [dma((OWNERS,))] * 8,
        compiler_params=pltpu.CompilerParams(
            collective_id=0, has_side_effects=True, vmem_limit_bytes=60 * 2**20),
        cost_estimate=pl.CostEstimate(
            flops=2 * rows * (PER + PICKS) * width, bytes_accessed=2 * rows * width, transcendentals=0),
    )(cand_index.reshape(-1, 128), pick_index.reshape(1, PICKS), embeddings)
    return lax.cond(
        flag[0, 0] == 0,
        lambda: (gains.reshape(PER), cover.reshape(rows)),
        lambda: whole_path(embeddings, pick_index, cand_index),
    )


def solution(mesh):
    return jax.shard_map(
        per_device,
        mesh=mesh,
        in_specs=(P("row", None), P(), P()),
        out_specs=(P("cand"), P("row")),
        check_vma=False,
    )
```

```python
import functools

import jax
import jax.numpy as jnp
from jax import lax
from jax.experimental import pallas as pl
from jax.experimental.pallas import tpu as pltpu
from jax.sharding import PartitionSpec as P

MESH = pl.DeviceIdType.MESH
F32 = jnp.float32
BF16 = jnp.bfloat16

CHIPS = ((0, 0), (1, 0), (0, 1), (0, 3), (1, 1), (1, 3), (0, 2), (1, 2))
ORDER = tuple((dz, dy, dc) for dz, dy in CHIPS for dc in (0, 1))
SLOT = {rel: j for j, rel in enumerate(ORDER)}
OWNERS = 16
PER = 1024
PICKS = 64
PCAP = 16
UNIT = 48
REST = 272
PICK_AT = 2 * UNIT
REST_AT = OWNERS * UNIT + PICKS
STREAM = REST_AT + REST
PASSES = ((0, PICK_AT, 2048), (PICK_AT, 448, 2048), (448, 736, 2048), (736, STREAM, 8192))


def unit_at(j):
    return UNIT * j + (PICKS if j >= 2 else 0)


def iota(shape, dim):
    return lax.broadcasted_iota(jnp.int32, shape, dim)


def dot(a, b):
    return jnp.dot(a, b, preferred_element_type=F32)


def inner(left, right):
    return lax.dot_general(left, right, (((1,), (1,)), ((), ())), preferred_element_type=F32)


def ones_where(cond):
    return jnp.where(cond, 1.0, 0.0).astype(BF16)


def order_of(owner, device):
    dz = (owner >> 3) ^ (device >> 3)
    dy = ((owner >> 1) - (device >> 1)) & 3
    chip = dz * 4 + dy
    place = jnp.zeros_like(chip)
    for rank, (cz, cy) in enumerate(CHIPS):
        place = jnp.where(chip == cz * 4 + cy, rank, place)
    return place * 2 + ((owner ^ device) & 1)


def kernel(
    shift,
    cand_hbm, pick_hbm, emb_hbm,
    gains_ref, cover_hbm, flag_ref,
    cand_ref, pick_ref, emb, ch, late, pk, pack, raw, cover_ref, acc, red,
    in_sem, load_sem, pk_send, pk_recv, ch_send, ch_recv, late_send, late_recv, red_send, red_recv,
):
    rows = emb.shape[0]
    width = emb.shape[1]
    chunks = load_sem.shape[0]
    chunk = rows // chunks
    me = lax.axis_index("row")
    group = lax.axis_index("cand")
    z, y, c = me // 8, (me // 2) % 4, me % 2

    def device(dz, dy, dc):
        return (z + dz) % 2 * 8 + (y + dy) % 4 * 2 + (c + dc) % 2

    def load(i):
        at = pl.ds(pl.multiple_of(i * chunk, chunk), chunk)
        return pltpu.make_async_copy(emb_hbm.at[at], emb.at[at], load_sem.at[i])

    cand_in = pltpu.make_async_copy(cand_hbm, cand_ref, in_sem.at[0])
    pick_in = pltpu.make_async_copy(pick_hbm, pick_ref, in_sem.at[1])
    cover_out = pltpu.make_async_copy(cover_ref, cover_hbm, in_sem.at[2])
    cand_in.start()
    pick_in.start()
    for i in range(chunks):
        load(i).start()

    barrier = pltpu.get_barrier_semaphore()
    for rel in ORDER[1:]:
        pl.semaphore_signal(barrier, inc=1, device_id={"row": device(*rel)}, device_id_type=MESH)
    cand_in.wait()
    pick_in.wait()

    mine = cand_ref[pl.ds(pl.multiple_of(group * 8, 8), 8), :]
    owner, local = mine >> shift, mine & (rows - 1)
    masks = [owner == device(*rel) for rel in ORDER]
    mask = jnp.concatenate([jnp.where(m, 1.0, 0.0) for m in masks], axis=0).astype(BF16)
    r0, r1 = iota((128, 128), 0), iota((128, 128), 1)
    before = ones_where(r0 < r1)
    within = dot(mask, before)
    totals = dot(mask, jnp.ones((128, 128), BF16)).astype(BF16)
    same = (r0 >> 3) == (r1 >> 3)
    rank = within + dot(ones_where(same & (r1 < r0)), totals)

    slots = iota((2 * UNIT, 128), 0).astype(F32)
    key = jnp.where(masks[0], rank[:8], -1.0)
    local_plus = (local + 1).astype(F32)
    slot_row = jnp.zeros((2 * UNIT, 128), F32)
    for r in range(8):
        slot_row += jnp.where(slots == key[r:r + 1], local_plus[r:r + 1], 0.0)
    cand_at = jnp.sum(slot_row, axis=1, keepdims=True)
    pick = pick_ref[...]
    pick_mine = (pick >> shift) == me
    pick_rank = dot(ones_where(jnp.broadcast_to(pick_mine, (8, PICKS))), before[:PICKS, :PICKS])
    pick_key = jnp.where(pick_mine, pick_rank[:1], -1.0)
    pick_plus = ((pick & (rows - 1)) + 1).astype(F32)
    pick_at = jnp.sum(
        jnp.where(iota((PCAP, PICKS), 0).astype(F32) == pick_key, pick_plus, 0.0), axis=1, keepdims=True)
    held_rows = 2 * UNIT + PCAP
    at_row = jnp.concatenate([cand_at, pick_at], axis=0).astype(jnp.int32) - 1
    at_row = jnp.broadcast_to(at_row, (held_rows, chunk))

    lanes = iota((held_rows, chunk), 1)

    def gather(i, total):
        load(i).wait()
        at = pl.ds(pl.multiple_of(i * chunk, chunk), chunk)
        return total + dot(ones_where(at_row - i * chunk == lanes), emb[at, :])

    total = lax.fori_loop(0, chunks, gather, jnp.zeros((held_rows, width), F32))
    pk[0] = total[2 * UNIT:].astype(BF16)
    ch[:UNIT] = total[:UNIT].astype(BF16)
    late[0] = total[UNIT:2 * UNIT].astype(BF16)

    pl.semaphore_wait(barrier, OWNERS - 1)

    def remote(src, dst, send_sem, recv_sem, to):
        return pltpu.make_async_remote_copy(
            src_ref=src, dst_ref=dst, send_sem=send_sem, recv_sem=recv_sem,
            device_id={"row": to}, device_id_type=MESH)

    def ch_block(j):
        return ch.at[pl.ds(unit_at(j), UNIT)]

    def late_block(j):
        return late.at[j]

    def pk_block(j):
        return pk.at[j]

    CH = (ch_block, ch_send, ch_recv)
    LATE = (late_block, late_send, late_recv)
    PK = (pk_block, pk_send, pk_recv)

    def own(part, rel):
        block, sent, got = part
        dz, dy, dc = rel
        to = SLOT[dz, -dy % 4, dc]
        return remote(block(0), block(to), sent.at[SLOT[rel]], got.at[to], device(*rel))

    def hand(part, chip):
        block, sent, got = part
        j = SLOT[(*chip, 0)]
        return remote(block(j), block(j + 1), sent.at[j + 1], got.at[j + 1], device(0, 0, 1))

    def moved(part, src, to, device_to):
        block, sent, got = part
        if part is CH:
            ref = ch.at[pl.ds(pl.multiple_of(src * UNIT + PICKS, 16), UNIT)]
        else:
            ref = block(src)
        return remote(ref, block(to), sent.at[to], got.at[to], device_to)

    def relay(part, dz):
        return moved(part, SLOT[dz, 3, 0] - 2 * c, SLOT[dz, 2, 0], device(0, 1 + 2 * c, 0))

    def across(part, dy):
        along_y = SLOT[0, dy, 0]
        src = along_y - c * (along_y - SLOT[1, 0, 0])
        return moved(part, src, SLOT[1, dy, 0], device(1 - c, c * (-dy % 4), 0))

    def arrived(part, *js):
        block, sent, got = part
        for j in js:
            remote(block(0), block(j), sent.at[j], got.at[j], device(0, 0, 1)).wait_recv()

    SIB = (0, 0, 1)
    NEAR = ((1, 0), (0, 1), (0, 3))
    DIAG = ((1, 1), (1, 3))
    FAR = ((0, 2), (1, 2))

    def evens(chips):
        return [SLOT[(*chip, 0)] for chip in chips]

    def odds(chips):
        return [SLOT[(*chip, 1)] for chip in chips]

    for chip in NEAR:
        own(CH, (*chip, 0)).start()
    own(CH, SIB).start()
    for chip in FAR + DIAG + NEAR:
        own(PK, (*chip, 0)).start()
    own(PK, SIB).start()

    held = jnp.zeros((8, 128), F32)
    every = cand_ref[...] >> shift
    lane8 = iota((8, 128), 1)
    for o in range(OWNERS):
        hit = jnp.where(every == o, 1.0, 0.0).reshape(8, 8, 128).sum(axis=1)
        held = jnp.where(lane8 == o, jnp.sum(hit, axis=1, keepdims=True), held)
    over = jnp.maximum(held - UNIT, 0.0)
    bad = (over > UNIT) | (jnp.sum(over, axis=1, keepdims=True) > REST)
    eye = iota((PICKS, PICKS), 0) == iota((PICKS, PICKS), 1)
    pick_col = jnp.sum(jnp.where(eye, (pick >> shift).astype(F32), 0.0), axis=1, keepdims=True).astype(jnp.int32)
    pick_hit = jnp.where(pick_col == iota((PICKS, 128), 1), 1.0, 0.0)
    pick_over = jnp.sum(pick_hit, axis=0, keepdims=True) > PCAP
    worst = jnp.maximum(jnp.max(jnp.where(bad, 1.0, 0.0)), jnp.max(jnp.where(pick_over, 1.0, 0.0)))
    flag_ref[0, 0] = worst.astype(jnp.int32)

    count = dot(ones_where(same), totals)
    rest = jnp.maximum(count - UNIT, 0.0).astype(BF16)
    rest_base = dot(ones_where(((r1 >> 3) < (r0 >> 3)) & ((r1 & 7) == 0)), rest)
    place = jnp.zeros((8, 128), F32)
    for j in range(OWNERS):
        at = slice(8 * j, 8 * j + 8)
        row = jnp.where(rank[at] < UNIT, rank[at] + unit_at(j), rank[at] + (rest_base[at] + (REST_AT - UNIT)))
        place += jnp.where(masks[j], row, 0.0)

    pick_order = order_of(pick_col, me)
    pick_one = ones_where(pick_order == iota((PICKS, 128), 1))
    earlier = dot(ones_where(iota((PICKS, PICKS), 1) < iota((PICKS, PICKS), 0)), pick_one)
    pick_rank_col = jnp.sum(jnp.where(pick_order == iota((PICKS, 128), 1), earlier, 0.0), axis=1, keepdims=True)
    pick_slot = pick_order * PCAP + pick_rank_col.astype(jnp.int32)
    pick_pack = ones_where(pick_slot == iota((PICKS, OWNERS * PCAP), 1))
    group_over = jnp.where(iota((8, 128), 0) == group, over, 0.0).astype(BF16)
    late_slots = OWNERS * UNIT
    block_of = (iota((128, late_slots), 1) * 1366) >> 16
    order_col = order_of(iota((128, late_slots), 0), me)
    order_col = jnp.where(iota((128, late_slots), 0) < OWNERS, order_col, OWNERS)
    late_base = jnp.sum(dot(group_over, ones_where(order_col < block_of)), axis=0, keepdims=True)
    late_count = jnp.sum(dot(group_over, ones_where(order_col == block_of)), axis=0, keepdims=True)
    late_slot = (iota((1, late_slots), 1) - block_of[:1] * UNIT).astype(F32)
    late_row = jnp.where(late_slot < late_count, late_base + late_slot, -1.0)

    def gain_of(get, covers, lo, hi):
        for top in range(lo, hi, 64):
            end = min(top + 64, hi)
            part = acc[top:end]
            for k, cover in enumerate(covers):
                part += jnp.maximum(get(top, end, k) - cover, 0.0)
            acc[top:end] = part

    def one_pass(t, polls):
        lo, hi, step_rows = PASSES[t]
        groups = step_rows // 128

        def step(i, carry):
            at = pl.multiple_of(i * step_rows, step_rows)
            s = inner(ch[lo:hi], emb[pl.ds(at, step_rows), :])

            def kept(top, end, k):
                return raw[top:end, pl.ds(pl.multiple_of(at + 128 * k, 128), 128)]

            def new(top, end, k):
                return s[top - lo:end - lo, 128 * k:128 * k + 128]

            if t == 0:
                raw[:, pl.ds(at, step_rows)] = s
            elif t == 1:
                cover = jnp.max(s[:PICKS], axis=0, keepdims=True)
                covers = [cover[:, 128 * k:128 * k + 128] for k in range(groups)]
                for k in range(groups):
                    cover_ref[pl.ds(i * groups + k, 1), :] = covers[k]
                gain_of(kept, covers, 0, PICK_AT)
                gain_of(new, covers, PICK_AT + PICKS, hi)
            else:
                covers = [cover_ref[pl.ds(i * groups + k, 1), :] for k in range(groups)]
                gain_of(new, covers, lo, hi)
            for n, todo in polls.items():
                @pl.when(i == n)
                def _(todo=todo):
                    for act in todo:
                        act()
            return carry

        lax.fori_loop(0, rows // step_rows, step, 0)

    def in_place(lo, hi):
        found = jnp.sum(acc[lo:hi], axis=1, keepdims=True)
        row = (iota((hi - lo, 128), 0) + lo).astype(F32)
        parts = [
            jnp.sum(jnp.where(row == place[r:r + 1], found, 0.0), axis=0, keepdims=True) for r in range(8)
        ]
        return jnp.concatenate(parts, axis=0)

    def hand_all(part, chips):
        arrived(part, *evens(chips))
        for chip in chips:
            hand(part, chip).start()

    def near(part):
        arrived(part, *evens(NEAR))
        for dy in (1, 3):
            across(part, dy).start()
        relay(part, 0).start()
        for chip in NEAR:
            hand(part, chip).start()

    def diagonal(part):
        arrived(part, *evens(DIAG))
        relay(part, 1).start()
        for chip in DIAG:
            hand(part, chip).start()

    def send_late():
        for chip in NEAR:
            own(LATE, (*chip, 0)).start()
        own(LATE, SIB).start()

    acc[...] = jnp.zeros((STREAM, 128), F32)
    pack[...] = ones_where(iota((REST, late_slots), 0).astype(F32) == late_row)
    arrived(CH, SLOT[SIB])
    one_pass(0, {2: [lambda: near(CH), send_late, lambda: hand_all(PK, NEAR + DIAG)]})
    hand_all(PK, FAR)
    arrived(CH, *odds(NEAR))
    arrived(PK, *range(1, OWNERS, 2))
    ch[PICK_AT:PICK_AT + PICKS] = dot(pick_pack, pk[...].reshape(OWNERS * PCAP, width)).astype(BF16)
    one_pass(1, {
        0: [lambda: diagonal(CH)],
        1: [lambda: near(LATE), lambda: hand_all(CH, FAR[:1])],
        3: [lambda: hand_all(CH, FAR[1:]), lambda: diagonal(LATE)],
    })
    cover_out.start()
    arrived(CH, *odds(DIAG + FAR[:1]))
    one_pass(2, {
        0: [lambda: hand_all(LATE, FAR[:1])],
        2: [lambda: hand_all(LATE, FAR[1:])],
    })
    red[me] = in_place(0, PASSES[3][0])
    arrived(CH, *odds(FAR[1:]))
    arrived(LATE, *range(1, OWNERS, 2))
    packed = dot(pack[...], late[...].reshape(late_slots, width))
    ch[REST_AT:] = packed.astype(BF16)
    one_pass(3, {})

    red[me] += in_place(PASSES[3][0], STREAM)

    def share(rel, at):
        return remote(red.at[me], red.at[at], red_send.at[SLOT[rel]], red_recv.at[at], device(*rel))

    for rel in ORDER[:0:-1]:
        share(rel, me).start()
    for rel in ORDER[1:]:
        share(rel, device(*rel)).wait_recv()
    whole = red[0]
    for o in range(1, OWNERS):
        whole += red[o]
    gains_ref[...] = whole * (1.0 / (rows * OWNERS))

    cover_out.wait()
    for rel in ORDER[1:]:
        share(rel, me).wait_send()
    for part in (PK, CH, LATE):
        own(part, SIB).wait_send()
        for chip in NEAR + DIAG + FAR:
            if part is PK or chip in NEAR:
                own(part, (*chip, 0)).wait_send()
            elif chip in DIAG:
                across(part, chip[1]).wait_send()
            else:
                relay(part, chip[0]).wait_send()
            hand(part, chip).wait_send()


def select_owned(embeddings, indices):
    count = embeddings.shape[0]
    local = indices - lax.axis_index("row") * count
    owned = (local >= 0) & (local < count)
    taken = jnp.take(embeddings, jnp.clip(local, 0, count - 1), axis=0)
    return jnp.where(owned[:, None], taken, jnp.zeros_like(taken))


def sum_over_rows(x):
    size = lax.axis_size("row")
    step = 1
    while step < size:
        x = x + lax.ppermute(x, "row", [(i, i ^ step) for i in range(size)])
        step *= 2
    return x


def whole_path(embeddings, pick_index, cand_index):
    count = embeddings.shape[0]
    per = cand_index.shape[0] // lax.axis_size("cand")
    mine = lax.dynamic_slice_in_dim(cand_index, lax.axis_index("cand") * per, per, 0)
    picked = sum_over_rows(select_owned(embeddings, pick_index))
    coverage = jnp.max(inner(embeddings, picked), axis=1)
    chosen = sum_over_rows(select_owned(embeddings, mine))
    similar = inner(embeddings, chosen)
    partial = jnp.sum(jnp.maximum(similar - coverage[:, None], 0.0), axis=0)
    return sum_over_rows(partial) / (count * lax.axis_size("row")), coverage


def settle(gains, cover, gains_out, cover_out, sem):
    copies = [
        pltpu.make_async_copy(gains, gains_out, sem.at[0]),
        pltpu.make_async_copy(cover, cover_out, sem.at[1]),
    ]
    for copy in copies:
        copy.start()
    for copy in copies:
        copy.wait()


def per_device(embeddings, pick_index, cand_index):
    rows, width = embeddings.shape
    shift = rows.bit_length() - 1
    chunks = 4
    anywhere = pl.BlockSpec(memory_space=pl.ANY)
    dma = pltpu.SemaphoreType.DMA
    gains, cover, flag = pl.pallas_call(
        functools.partial(kernel, shift),
        out_shape=[
            jax.ShapeDtypeStruct((8, 128), F32),
            jax.ShapeDtypeStruct((rows // 128, 128), F32),
            jax.ShapeDtypeStruct((1, 1), jnp.int32),
        ],
        in_specs=[anywhere, anywhere, anywhere],
        out_specs=[pl.BlockSpec(memory_space=pltpu.VMEM), anywhere, pl.BlockSpec(memory_space=pltpu.SMEM)],
        scratch_shapes=[
            pltpu.VMEM((64, 128), jnp.int32),
            pltpu.VMEM((1, PICKS), jnp.int32),
            pltpu.VMEM((rows, width), BF16),
            pltpu.VMEM((STREAM, width), BF16),
            pltpu.VMEM((OWNERS, UNIT, width), BF16),
            pltpu.VMEM((OWNERS, PCAP, width), BF16),
            pltpu.VMEM((REST, OWNERS * UNIT), BF16),
            pltpu.VMEM((PICK_AT, rows), F32),
            pltpu.VMEM((rows // 128, 128), F32),
            pltpu.VMEM((STREAM, 128), F32),
            pltpu.VMEM((OWNERS, 8, 128), F32),
            dma((3,)), dma((chunks,)),
        ] + [dma((OWNERS,))] * 8,
        compiler_params=pltpu.CompilerParams(
            collective_id=0, has_side_effects=True, vmem_limit_bytes=60 * 2**20),
        cost_estimate=pl.CostEstimate(
            flops=2 * rows * (PER + PICKS) * width, bytes_accessed=2 * rows * width, transcendentals=0),
    )(cand_index.reshape(-1, 128), pick_index.reshape(1, PICKS), embeddings)

    def fast_path():
        in_hbm = pl.BlockSpec(memory_space=pltpu.HBM)
        outs = pl.pallas_call(
            settle,
            out_shape=[jax.ShapeDtypeStruct(x.shape, F32) for x in (gains, cover)],
            in_specs=[anywhere] * 2, out_specs=[in_hbm] * 2, scratch_shapes=[dma((2,))],
        )(gains, cover)
        return outs[0].reshape(PER), outs[1].reshape(rows)

    return lax.cond(
        flag[0, 0] == 0, fast_path, lambda: whole_path(embeddings, pick_index, cand_index))


def solution(mesh):
    return jax.shard_map(
        per_device,
        mesh=mesh,
        in_specs=(P("row", None), P(), P()),
        out_specs=(P("cand"), P("row")),
        check_vma=False,
    )
```

```python
import functools

import jax
import jax.numpy as jnp
from jax import lax
from jax.experimental import pallas as pl
from jax.experimental.pallas import tpu as pltpu
from jax.sharding import PartitionSpec as P

MESH = pl.DeviceIdType.MESH
F32 = jnp.float32
BF16 = jnp.bfloat16

CHIPS = ((0, 0), (1, 0), (0, 1), (0, 3), (1, 1), (1, 3), (0, 2), (1, 2))
ORDER = tuple((dz, dy, dc) for dz, dy in CHIPS for dc in (0, 1))
SLOT = {rel: j for j, rel in enumerate(ORDER)}
OWNERS = 16
PER = 1024
PICKS = 64
PCAP = 16
UNIT = 48
REST = 272
PICK_AT = 2 * UNIT
REST_AT = OWNERS * UNIT + PICKS
STREAM = REST_AT + REST
PASSES = ((0, PICK_AT, 2048), (PICK_AT, 448, 4096), (448, 736, 4096), (736, STREAM, 8192))


def unit_at(j):
    return UNIT * j + (PICKS if j >= 2 else 0)


def iota(shape, dim):
    return lax.broadcasted_iota(jnp.int32, shape, dim)


def dot(a, b):
    return jnp.dot(a, b, preferred_element_type=F32)


def inner(left, right):
    return lax.dot_general(left, right, (((1,), (1,)), ((), ())), preferred_element_type=F32)


def ones_where(cond):
    return jnp.where(cond, 1.0, 0.0).astype(BF16)


def order_of(owner, device):
    dz = (owner >> 3) ^ (device >> 3)
    dy = ((owner >> 1) - (device >> 1)) & 3
    chip = dz * 4 + dy
    place = jnp.zeros_like(chip)
    for rank, (cz, cy) in enumerate(CHIPS):
        place = jnp.where(chip == cz * 4 + cy, rank, place)
    return place * 2 + ((owner ^ device) & 1)


def kernel(
    shift,
    cand_hbm, pick_hbm, emb_hbm,
    gains_ref, cover_hbm, flag_ref,
    cand_ref, pick_ref, emb, ch, late, pk, pack, raw, cover_ref, acc, red,
    in_sem, load_sem, pk_send, pk_recv, ch_send, ch_recv, late_send, late_recv, red_send, red_recv,
):
    rows = emb.shape[0]
    width = emb.shape[1]
    chunks = load_sem.shape[0]
    chunk = rows // chunks
    me = lax.axis_index("row")
    group = lax.axis_index("cand")
    z, y, c = me // 8, (me // 2) % 4, me % 2

    def device(dz, dy, dc):
        return (z + dz) % 2 * 8 + (y + dy) % 4 * 2 + (c + dc) % 2

    def load(i):
        at = pl.ds(pl.multiple_of(i * chunk, chunk), chunk)
        return pltpu.make_async_copy(emb_hbm.at[at], emb.at[at], load_sem.at[i])

    cand_in = pltpu.make_async_copy(cand_hbm, cand_ref, in_sem.at[0])
    pick_in = pltpu.make_async_copy(pick_hbm, pick_ref, in_sem.at[1])
    cover_out = pltpu.make_async_copy(cover_ref, cover_hbm, in_sem.at[2])
    cand_in.start()
    pick_in.start()
    for i in range(2):
        load(i).start()

    barrier = pltpu.get_barrier_semaphore()
    for rel in ORDER[1:]:
        pl.semaphore_signal(barrier, inc=1, device_id={"row": device(*rel)}, device_id_type=MESH)
    cand_in.wait()
    pick_in.wait()

    mine = cand_ref[pl.ds(pl.multiple_of(group * 8, 8), 8), :]
    owner, local = mine >> shift, mine & (rows - 1)
    masks = [owner == device(*rel) for rel in ORDER]
    mask = jnp.concatenate([jnp.where(m, 1.0, 0.0) for m in masks], axis=0).astype(BF16)
    r0, r1 = iota((128, 128), 0), iota((128, 128), 1)
    before = ones_where(r0 < r1)
    within = dot(mask, before)
    totals = dot(mask, jnp.ones((128, 128), BF16)).astype(BF16)
    same = (r0 >> 3) == (r1 >> 3)
    rank = within + dot(ones_where(same & (r1 < r0)), totals)

    slots = iota((2 * UNIT, 128), 0).astype(F32)
    key = jnp.where(masks[0], rank[:8], -1.0)
    local_plus = (local + 1).astype(F32)
    slot_row = jnp.zeros((2 * UNIT, 128), F32)
    for r in range(8):
        slot_row += jnp.where(slots == key[r:r + 1], local_plus[r:r + 1], 0.0)
    cand_at = jnp.sum(slot_row, axis=1, keepdims=True)
    pick = pick_ref[...]
    pick_mine = (pick >> shift) == me
    pick_rank = dot(ones_where(jnp.broadcast_to(pick_mine, (8, PICKS))), before[:PICKS, :PICKS])
    pick_key = jnp.where(pick_mine, pick_rank[:1], -1.0)
    pick_plus = ((pick & (rows - 1)) + 1).astype(F32)
    pick_at = jnp.sum(
        jnp.where(iota((PCAP, PICKS), 0).astype(F32) == pick_key, pick_plus, 0.0), axis=1, keepdims=True)
    held_rows = 2 * UNIT + PCAP
    at_row = jnp.concatenate([cand_at, pick_at], axis=0).astype(jnp.int32) - 1
    at_row = jnp.broadcast_to(at_row, (held_rows, chunk))

    lanes = iota((held_rows, chunk), 1)

    def gather(i, total):
        load(i).wait()

        @pl.when(i + 2 < chunks)
        def _():
            load(i + 2).start()

        at = pl.ds(pl.multiple_of(i * chunk, chunk), chunk)
        return total + dot(ones_where(at_row - i * chunk == lanes), emb[at, :])

    total = lax.fori_loop(0, chunks, gather, jnp.zeros((held_rows, width), F32))
    pk[0] = total[2 * UNIT:].astype(BF16)
    ch[:UNIT] = total[:UNIT].astype(BF16)
    late[0] = total[UNIT:2 * UNIT].astype(BF16)

    pl.semaphore_wait(barrier, OWNERS - 1)

    def remote(src, dst, send_sem, recv_sem, to):
        return pltpu.make_async_remote_copy(
            src_ref=src, dst_ref=dst, send_sem=send_sem, recv_sem=recv_sem,
            device_id={"row": to}, device_id_type=MESH)

    def ch_block(j):
        return ch.at[pl.ds(unit_at(j), UNIT)]

    def late_block(j):
        return late.at[j]

    def pk_block(j):
        return pk.at[j]

    CH = (ch_block, ch_send, ch_recv)
    LATE = (late_block, late_send, late_recv)
    PK = (pk_block, pk_send, pk_recv)

    def own(part, rel):
        block, sent, got = part
        dz, dy, dc = rel
        to = SLOT[dz, -dy % 4, dc]
        return remote(block(0), block(to), sent.at[SLOT[rel]], got.at[to], device(*rel))

    def hand(part, chip):
        block, sent, got = part
        j = SLOT[(*chip, 0)]
        return remote(block(j), block(j + 1), sent.at[j + 1], got.at[j + 1], device(0, 0, 1))

    def moved(part, src, to, device_to):
        block, sent, got = part
        if part is CH:
            ref = ch.at[pl.ds(pl.multiple_of(src * UNIT + PICKS, 16), UNIT)]
        else:
            ref = block(src)
        return remote(ref, block(to), sent.at[to], got.at[to], device_to)

    def relay(part, dz):
        return moved(part, SLOT[dz, 3, 0] - 2 * c, SLOT[dz, 2, 0], device(0, 1 + 2 * c, 0))

    def across(part, dy):
        along_y = SLOT[0, dy, 0]
        src = along_y - c * (along_y - SLOT[1, 0, 0])
        return moved(part, src, SLOT[1, dy, 0], device(1 - c, c * (-dy % 4), 0))

    def arrived(part, *js):
        block, sent, got = part
        for j in js:
            remote(block(0), block(j), sent.at[j], got.at[j], device(0, 0, 1)).wait_recv()

    STRAIGHT = (PK, LATE)
    SIB = (0, 0, 1)
    NEAR = ((1, 0), (0, 1), (0, 3))
    DIAG = ((1, 1), (1, 3))
    FAR = ((0, 2), (1, 2))

    def evens(chips):
        return [SLOT[(*chip, 0)] for chip in chips]

    def odds(chips):
        return [SLOT[(*chip, 1)] for chip in chips]

    for chip in NEAR:
        own(CH, (*chip, 0)).start()
    own(CH, SIB).start()
    if CH in STRAIGHT:
        own(CH, (*FAR[1], 0)).start()
    for chip in FAR + DIAG + NEAR:
        own(PK, (*chip, 0)).start()
    own(PK, SIB).start()

    held = jnp.zeros((8, 128), F32)
    every = cand_ref[...] >> shift
    lane8 = iota((8, 128), 1)
    for o in range(OWNERS):
        hit = jnp.where(every == o, 1.0, 0.0).reshape(8, 8, 128).sum(axis=1)
        held = jnp.where(lane8 == o, jnp.sum(hit, axis=1, keepdims=True), held)
    over = jnp.maximum(held - UNIT, 0.0)
    bad = (over > UNIT) | (jnp.sum(over, axis=1, keepdims=True) > REST)
    eye = iota((PICKS, PICKS), 0) == iota((PICKS, PICKS), 1)
    pick_col = jnp.sum(jnp.where(eye, (pick >> shift).astype(F32), 0.0), axis=1, keepdims=True).astype(jnp.int32)
    pick_hit = jnp.where(pick_col == iota((PICKS, 128), 1), 1.0, 0.0)
    pick_over = jnp.sum(pick_hit, axis=0, keepdims=True) > PCAP
    worst = jnp.maximum(jnp.max(jnp.where(bad, 1.0, 0.0)), jnp.max(jnp.where(pick_over, 1.0, 0.0)))
    flag_ref[0, 0] = worst.astype(jnp.int32)

    count = dot(ones_where(same), totals)
    rest = jnp.maximum(count - UNIT, 0.0).astype(BF16)
    rest_base = dot(ones_where(((r1 >> 3) < (r0 >> 3)) & ((r1 & 7) == 0)), rest)
    place = jnp.zeros((8, 128), F32)
    for j in range(OWNERS):
        at = slice(8 * j, 8 * j + 8)
        row = jnp.where(rank[at] < UNIT, rank[at] + unit_at(j), rank[at] + (rest_base[at] + (REST_AT - UNIT)))
        place += jnp.where(masks[j], row, 0.0)

    pick_order = order_of(pick_col, me)
    pick_one = ones_where(pick_order == iota((PICKS, 128), 1))
    earlier = dot(ones_where(iota((PICKS, PICKS), 1) < iota((PICKS, PICKS), 0)), pick_one)
    pick_rank_col = jnp.sum(jnp.where(pick_order == iota((PICKS, 128), 1), earlier, 0.0), axis=1, keepdims=True)
    pick_slot = pick_order * PCAP + pick_rank_col.astype(jnp.int32)
    pick_pack = ones_where(pick_slot == iota((PICKS, OWNERS * PCAP), 1))
    group_over = jnp.where(iota((8, 128), 0) == group, over, 0.0).astype(BF16)
    late_slots = OWNERS * UNIT
    block_of = (iota((128, late_slots), 1) * 1366) >> 16
    order_col = order_of(iota((128, late_slots), 0), me)
    order_col = jnp.where(iota((128, late_slots), 0) < OWNERS, order_col, OWNERS)
    late_base = jnp.sum(dot(group_over, ones_where(order_col < block_of)), axis=0, keepdims=True)
    late_count = jnp.sum(dot(group_over, ones_where(order_col == block_of)), axis=0, keepdims=True)
    late_slot = (iota((1, late_slots), 1) - block_of[:1] * UNIT).astype(F32)
    late_row = jnp.where(late_slot < late_count, late_base + late_slot, -1.0)

    def gain_of(get, covers, lo, hi):
        for top in range(lo, hi, 64):
            end = min(top + 64, hi)
            part = acc[top:end]
            for k, cover in enumerate(covers):
                part += jnp.maximum(get(top, end, k) - cover, 0.0)
            acc[top:end] = part

    def one_pass(t, polls):
        lo, hi, step_rows = PASSES[t]
        groups = step_rows // 128

        def step(i, carry):
            at = pl.multiple_of(i * step_rows, step_rows)
            s = inner(ch[lo:hi], emb[pl.ds(at, step_rows), :])

            def kept(top, end, k):
                return raw[top:end, pl.ds(pl.multiple_of(at + 128 * k, 128), 128)]

            def new(top, end, k):
                return s[top - lo:end - lo, 128 * k:128 * k + 128]

            if t == 0:
                raw[:, pl.ds(at, step_rows)] = s
            elif t == 1:
                cover = jnp.max(s[:PICKS], axis=0, keepdims=True)
                covers = [cover[:, 128 * k:128 * k + 128] for k in range(groups)]
                for k in range(groups):
                    cover_ref[pl.ds(i * groups + k, 1), :] = covers[k]
                gain_of(kept, covers, 0, PICK_AT)
                gain_of(new, covers, PICK_AT + PICKS, hi)
            else:
                covers = [cover_ref[pl.ds(i * groups + k, 1), :] for k in range(groups)]
                gain_of(new, covers, lo, hi)
            for n, todo in polls.items():
                @pl.when(i == n)
                def _(todo=todo):
                    for act in todo:
                        act()
            return carry

        lax.fori_loop(0, rows // step_rows, step, 0)

    def in_place(lo, hi):
        found = jnp.sum(acc[lo:hi], axis=1, keepdims=True)
        row = (iota((hi - lo, 128), 0) + lo).astype(F32)
        parts = [
            jnp.sum(jnp.where(row == place[r:r + 1], found, 0.0), axis=0, keepdims=True) for r in range(8)
        ]
        return jnp.concatenate(parts, axis=0)

    def hand_all(part, chips):
        arrived(part, *evens(chips))
        for chip in chips:
            hand(part, chip).start()

    def near(part):
        arrived(part, *evens(NEAR))
        for dy in (1, 3):
            across(part, dy).start()
        relay(part, 0).start()
        for chip in NEAR:
            hand(part, chip).start()

    def diagonal(part):
        arrived(part, *evens(DIAG))
        if part not in STRAIGHT:
            relay(part, 1).start()
        for chip in DIAG:
            hand(part, chip).start()

    def send_late():
        for chip in NEAR:
            own(LATE, (*chip, 0)).start()
        own(LATE, SIB).start()
        if LATE in STRAIGHT:
            own(LATE, (*FAR[1], 0)).start()

    acc[...] = jnp.zeros((STREAM, 128), F32)
    pack[...] = ones_where(iota((REST, late_slots), 0).astype(F32) == late_row)
    arrived(CH, SLOT[SIB])
    one_pass(0, {2: [lambda: near(CH), send_late, lambda: hand_all(PK, NEAR + DIAG)]})
    hand_all(PK, FAR)
    arrived(CH, *odds(NEAR))
    arrived(PK, *range(1, OWNERS, 2))
    ch[PICK_AT:PICK_AT + PICKS] = dot(pick_pack, pk[...].reshape(OWNERS * PCAP, width)).astype(BF16)
    one_pass(1, {
        0: [lambda: diagonal(CH), lambda: hand_all(CH, FAR[:1]), lambda: near(LATE)],
        1: [lambda: hand_all(CH, FAR[1:]), lambda: hand_all(LATE, FAR[1:])],
    })
    cover_out.start()
    arrived(CH, *odds(DIAG + FAR[:1]))
    one_pass(2, {0: [lambda: diagonal(LATE), lambda: hand_all(LATE, FAR[:1])]})
    red[me] = in_place(0, PASSES[3][0])
    arrived(CH, *odds(FAR[1:]))
    arrived(LATE, *range(1, OWNERS, 2))
    packed = dot(pack[...], late[...].reshape(late_slots, width))
    ch[REST_AT:] = packed.astype(BF16)
    one_pass(3, {})

    red[me] += in_place(PASSES[3][0], STREAM)

    def share(rel, at):
        return remote(red.at[me], red.at[at], red_send.at[SLOT[rel]], red_recv.at[at], device(*rel))

    for rel in ORDER[:0:-1]:
        share(rel, me).start()
    for rel in ORDER[1:]:
        share(rel, device(*rel)).wait_recv()
    whole = red[0]
    for o in range(1, OWNERS):
        whole += red[o]
    gains_ref[...] = whole * (1.0 / (rows * OWNERS))

    cover_out.wait()
    for rel in ORDER[1:]:
        share(rel, me).wait_send()
    for part in (PK, CH, LATE):
        own(part, SIB).wait_send()
        for chip in NEAR + DIAG + FAR:
            if part is PK or chip in NEAR or (chip == FAR[1] and part in STRAIGHT):
                own(part, (*chip, 0)).wait_send()
            elif chip in DIAG:
                across(part, chip[1]).wait_send()
            else:
                relay(part, chip[0]).wait_send()
            hand(part, chip).wait_send()


def select_owned(embeddings, indices):
    count = embeddings.shape[0]
    local = indices - lax.axis_index("row") * count
    owned = (local >= 0) & (local < count)
    taken = jnp.take(embeddings, jnp.clip(local, 0, count - 1), axis=0)
    return jnp.where(owned[:, None], taken, jnp.zeros_like(taken))


def sum_over_rows(x):
    size = lax.axis_size("row")
    step = 1
    while step < size:
        x = x + lax.ppermute(x, "row", [(i, i ^ step) for i in range(size)])
        step *= 2
    return x


def whole_path(embeddings, pick_index, cand_index):
    count = embeddings.shape[0]
    per = cand_index.shape[0] // lax.axis_size("cand")
    mine = lax.dynamic_slice_in_dim(cand_index, lax.axis_index("cand") * per, per, 0)
    picked = sum_over_rows(select_owned(embeddings, pick_index))
    coverage = jnp.max(inner(embeddings, picked), axis=1)
    chosen = sum_over_rows(select_owned(embeddings, mine))
    similar = inner(embeddings, chosen)
    partial = jnp.sum(jnp.maximum(similar - coverage[:, None], 0.0), axis=0)
    return sum_over_rows(partial) / (count * lax.axis_size("row")), coverage


def settle(gains, cover, gains_out, cover_out, sem):
    copies = [
        pltpu.make_async_copy(gains, gains_out, sem.at[0]),
        pltpu.make_async_copy(cover, cover_out, sem.at[1]),
    ]
    for copy in copies:
        copy.start()
    for copy in copies:
        copy.wait()


def per_device(embeddings, pick_index, cand_index):
    rows, width = embeddings.shape
    shift = rows.bit_length() - 1
    chunks = 4
    anywhere = pl.BlockSpec(memory_space=pl.ANY)
    dma = pltpu.SemaphoreType.DMA
    gains, cover, flag = pl.pallas_call(
        functools.partial(kernel, shift),
        out_shape=[
            jax.ShapeDtypeStruct((8, 128), F32),
            jax.ShapeDtypeStruct((rows // 128, 128), F32),
            jax.ShapeDtypeStruct((1, 1), jnp.int32),
        ],
        in_specs=[anywhere, anywhere, anywhere],
        out_specs=[pl.BlockSpec(memory_space=pltpu.VMEM), anywhere, pl.BlockSpec(memory_space=pltpu.SMEM)],
        scratch_shapes=[
            pltpu.VMEM((64, 128), jnp.int32),
            pltpu.VMEM((1, PICKS), jnp.int32),
            pltpu.VMEM((rows, width), BF16),
            pltpu.VMEM((STREAM, width), BF16),
            pltpu.VMEM((OWNERS, UNIT, width), BF16),
            pltpu.VMEM((OWNERS, PCAP, width), BF16),
            pltpu.VMEM((REST, OWNERS * UNIT), BF16),
            pltpu.VMEM((PICK_AT, rows), F32),
            pltpu.VMEM((rows // 128, 128), F32),
            pltpu.VMEM((STREAM, 128), F32),
            pltpu.VMEM((OWNERS, 8, 128), F32),
            dma((3,)), dma((chunks,)),
        ] + [dma((OWNERS,))] * 8,
        compiler_params=pltpu.CompilerParams(
            collective_id=0, has_side_effects=True, vmem_limit_bytes=60 * 2**20),
        cost_estimate=pl.CostEstimate(
            flops=2 * rows * (PER + PICKS) * width, bytes_accessed=2 * rows * width, transcendentals=0),
    )(cand_index.reshape(-1, 128), pick_index.reshape(1, PICKS), embeddings)

    def fast_path():
        in_hbm = pl.BlockSpec(memory_space=pltpu.HBM)
        outs = pl.pallas_call(
            settle,
            out_shape=[jax.ShapeDtypeStruct(x.shape, F32) for x in (gains, cover)],
            in_specs=[anywhere] * 2, out_specs=[in_hbm] * 2, scratch_shapes=[dma((2,))],
        )(gains, cover)
        return outs[0].reshape(PER), outs[1].reshape(rows)

    return lax.cond(
        flag[0, 0] == 0, fast_path, lambda: whole_path(embeddings, pick_index, cand_index))


def solution(mesh):
    return jax.shard_map(
        per_device,
        mesh=mesh,
        in_specs=(P("row", None), P(), P()),
        out_specs=(P("cand"), P("row")),
        check_vma=False,
    )
```

```python
import functools

import jax
import jax.numpy as jnp
from jax import lax
from jax.experimental import pallas as pl
from jax.experimental.pallas import tpu as pltpu
from jax.sharding import PartitionSpec as P

MESH = pl.DeviceIdType.MESH
F32 = jnp.float32
BF16 = jnp.bfloat16

CHIPS = ((0, 0), (1, 0), (0, 1), (0, 3), (1, 1), (1, 3), (0, 2), (1, 2))
ORDER = tuple((dz, dy, dc) for dz, dy in CHIPS for dc in (0, 1))
SLOT = {rel: j for j, rel in enumerate(ORDER)}
OWNERS = 16
PER = 1024
PICKS = 64
PCAP = 16
UNIT = 48
REST = 272
PICK_AT = 2 * UNIT
REST_AT = OWNERS * UNIT + PICKS
STREAM = REST_AT + REST
PASSES = ((0, PICK_AT, 2048), (PICK_AT, 448, 4096), (448, 736, 4096), (736, STREAM, 8192))


def unit_at(j):
    return UNIT * j + (PICKS if j >= 2 else 0)


def iota(shape, dim):
    return lax.broadcasted_iota(jnp.int32, shape, dim)


def dot(a, b):
    return jnp.dot(a, b, preferred_element_type=F32)


def inner(left, right):
    return lax.dot_general(left, right, (((1,), (1,)), ((), ())), preferred_element_type=F32)


def ones_where(cond):
    return jnp.where(cond, 1.0, 0.0).astype(BF16)


def order_of(owner, device):
    dz = (owner >> 3) ^ (device >> 3)
    dy = ((owner >> 1) - (device >> 1)) & 3
    chip = dz * 4 + dy
    place = jnp.zeros_like(chip)
    for rank, (cz, cy) in enumerate(CHIPS):
        place = jnp.where(chip == cz * 4 + cy, rank, place)
    return place * 2 + ((owner ^ device) & 1)


def kernel(
    shift,
    cand_hbm, pick_hbm, emb_hbm,
    gains_ref, cover_hbm, flag_ref,
    cand_ref, pick_ref, emb, ch, late, pk, pack, raw, cover_ref, acc, red,
    in_sem, load_sem, pk_send, pk_recv, ch_send, ch_recv, late_send, late_recv, red_send, red_recv,
):
    rows = emb.shape[0]
    width = emb.shape[1]
    chunks = load_sem.shape[0]
    chunk = rows // chunks
    me = lax.axis_index("row")
    group = lax.axis_index("cand")
    z, y, c = me // 8, (me // 2) % 4, me % 2

    def device(dz, dy, dc):
        return (z + dz) % 2 * 8 + (y + dy) % 4 * 2 + (c + dc) % 2

    def load(i):
        at = pl.ds(pl.multiple_of(i * chunk, chunk), chunk)
        return pltpu.make_async_copy(emb_hbm.at[at], emb.at[at], load_sem.at[i])

    cand_in = pltpu.make_async_copy(cand_hbm, cand_ref, in_sem.at[0])
    pick_in = pltpu.make_async_copy(pick_hbm, pick_ref, in_sem.at[1])
    cover_out = pltpu.make_async_copy(cover_ref, cover_hbm, in_sem.at[2])
    cand_in.start()
    pick_in.start()
    for i in range(2):
        load(i).start()

    barrier = pltpu.get_barrier_semaphore()
    for rel in ORDER[1:]:
        pl.semaphore_signal(barrier, inc=1, device_id={"row": device(*rel)}, device_id_type=MESH)
    cand_in.wait()
    pick_in.wait()

    mine = cand_ref[pl.ds(pl.multiple_of(group * 8, 8), 8), :]
    owner, local = mine >> shift, mine & (rows - 1)
    masks = [owner == device(*rel) for rel in ORDER]
    mask = jnp.concatenate([jnp.where(m, 1.0, 0.0) for m in masks], axis=0).astype(BF16)
    r0, r1 = iota((128, 128), 0), iota((128, 128), 1)
    before = ones_where(r0 < r1)
    within = dot(mask, before)
    totals = dot(mask, jnp.ones((128, 128), BF16)).astype(BF16)
    same = (r0 >> 3) == (r1 >> 3)
    rank = within + dot(ones_where(same & (r1 < r0)), totals)

    slots = iota((2 * UNIT, 128), 0).astype(F32)
    key = jnp.where(masks[0], rank[:8], -1.0)
    local_plus = (local + 1).astype(F32)
    slot_row = jnp.zeros((2 * UNIT, 128), F32)
    for r in range(8):
        slot_row += jnp.where(slots == key[r:r + 1], local_plus[r:r + 1], 0.0)
    cand_at = jnp.sum(slot_row, axis=1, keepdims=True)
    pick = pick_ref[...]
    pick_mine = (pick >> shift) == me
    pick_rank = dot(ones_where(jnp.broadcast_to(pick_mine, (8, PICKS))), before[:PICKS, :PICKS])
    pick_key = jnp.where(pick_mine, pick_rank[:1], -1.0)
    pick_plus = ((pick & (rows - 1)) + 1).astype(F32)
    pick_at = jnp.sum(
        jnp.where(iota((PCAP, PICKS), 0).astype(F32) == pick_key, pick_plus, 0.0), axis=1, keepdims=True)
    held_rows = 2 * UNIT + PCAP
    at_row = jnp.concatenate([cand_at, pick_at], axis=0).astype(jnp.int32) - 1
    at_row = jnp.broadcast_to(at_row, (held_rows, chunk))

    lanes = iota((held_rows, chunk), 1)

    def gather(i, total):
        load(i).wait()

        @pl.when(i + 2 < chunks)
        def _():
            load(i + 2).start()

        at = pl.ds(pl.multiple_of(i * chunk, chunk), chunk)
        return total + dot(ones_where(at_row - i * chunk == lanes), emb[at, :])

    total = lax.fori_loop(0, chunks, gather, jnp.zeros((held_rows, width), F32))
    pk[0] = total[2 * UNIT:].astype(BF16)
    ch[:UNIT] = total[:UNIT].astype(BF16)
    late[0] = total[UNIT:2 * UNIT].astype(BF16)

    pl.semaphore_wait(barrier, OWNERS - 1)

    def remote(src, dst, send_sem, recv_sem, to):
        return pltpu.make_async_remote_copy(
            src_ref=src, dst_ref=dst, send_sem=send_sem, recv_sem=recv_sem,
            device_id={"row": to}, device_id_type=MESH)

    def ch_block(j):
        return ch.at[pl.ds(unit_at(j), UNIT)]

    def late_block(j):
        return late.at[j]

    def pk_block(j):
        return pk.at[j]

    CH = (ch_block, ch_send, ch_recv)
    LATE = (late_block, late_send, late_recv)
    PK = (pk_block, pk_send, pk_recv)

    def own(part, rel):
        block, sent, got = part
        dz, dy, dc = rel
        to = SLOT[dz, -dy % 4, dc]
        return remote(block(0), block(to), sent.at[SLOT[rel]], got.at[to], device(*rel))

    def hand(part, chip):
        block, sent, got = part
        j = SLOT[(*chip, 0)]
        return remote(block(j), block(j + 1), sent.at[j + 1], got.at[j + 1], device(0, 0, 1))

    def moved(part, src, to, device_to):
        block, sent, got = part
        if part is CH:
            ref = ch.at[pl.ds(pl.multiple_of(src * UNIT + PICKS, 16), UNIT)]
        else:
            ref = block(src)
        return remote(ref, block(to), sent.at[to], got.at[to], device_to)

    def relay(part, dz):
        return moved(part, SLOT[dz, 3, 0] - 2 * c, SLOT[dz, 2, 0], device(0, 1 + 2 * c, 0))

    def across(part, dy):
        along_y = SLOT[0, dy, 0]
        src = along_y - c * (along_y - SLOT[1, 0, 0])
        return moved(part, src, SLOT[1, dy, 0], device(1 - c, c * (-dy % 4), 0))

    def arrived(part, *js):
        block, sent, got = part
        for j in js:
            remote(block(0), block(j), sent.at[j], got.at[j], device(0, 0, 1)).wait_recv()

    STRAIGHT = (PK, LATE)
    SIB = (0, 0, 1)
    NEAR = ((1, 0), (0, 1), (0, 3))
    DIAG = ((1, 1), (1, 3))
    FAR = ((0, 2), (1, 2))

    def evens(chips):
        return [SLOT[(*chip, 0)] for chip in chips]

    def odds(chips):
        return [SLOT[(*chip, 1)] for chip in chips]

    for chip in NEAR:
        own(CH, (*chip, 0)).start()
    own(CH, SIB).start()
    if CH in STRAIGHT:
        own(CH, (*FAR[1], 0)).start()
    for chip in FAR + DIAG + NEAR:
        own(PK, (*chip, 0)).start()
    own(PK, SIB).start()

    held = jnp.zeros((8, 128), F32)
    every = cand_ref[...] >> shift
    lane8 = iota((8, 128), 1)
    for o in range(OWNERS):
        hit = jnp.where(every == o, 1.0, 0.0).reshape(8, 8, 128).sum(axis=1)
        held = jnp.where(lane8 == o, jnp.sum(hit, axis=1, keepdims=True), held)
    over = jnp.maximum(held - UNIT, 0.0)
    bad = (over > UNIT) | (jnp.sum(over, axis=1, keepdims=True) > REST)
    eye = iota((PICKS, PICKS), 0) == iota((PICKS, PICKS), 1)
    pick_col = jnp.sum(jnp.where(eye, (pick >> shift).astype(F32), 0.0), axis=1, keepdims=True).astype(jnp.int32)
    pick_hit = jnp.where(pick_col == iota((PICKS, 128), 1), 1.0, 0.0)
    pick_over = jnp.sum(pick_hit, axis=0, keepdims=True) > PCAP
    worst = jnp.maximum(jnp.max(jnp.where(bad, 1.0, 0.0)), jnp.max(jnp.where(pick_over, 1.0, 0.0)))
    flag_ref[0, 0] = worst.astype(jnp.int32)

    count = dot(ones_where(same), totals)
    rest = jnp.maximum(count - UNIT, 0.0).astype(BF16)
    rest_base = dot(ones_where(((r1 >> 3) < (r0 >> 3)) & ((r1 & 7) == 0)), rest)
    place = jnp.zeros((8, 128), F32)
    for j in range(OWNERS):
        at = slice(8 * j, 8 * j + 8)
        row = jnp.where(rank[at] < UNIT, rank[at] + unit_at(j), rank[at] + (rest_base[at] + (REST_AT - UNIT)))
        place += jnp.where(masks[j], row, 0.0)

    pick_order = order_of(pick_col, me)
    pick_one = ones_where(pick_order == iota((PICKS, 128), 1))
    earlier = dot(ones_where(iota((PICKS, PICKS), 1) < iota((PICKS, PICKS), 0)), pick_one)
    pick_rank_col = jnp.sum(jnp.where(pick_order == iota((PICKS, 128), 1), earlier, 0.0), axis=1, keepdims=True)
    pick_slot = pick_order * PCAP + pick_rank_col.astype(jnp.int32)
    pick_pack = ones_where(pick_slot == iota((PICKS, OWNERS * PCAP), 1))
    group_over = jnp.where(iota((8, 128), 0) == group, over, 0.0).astype(BF16)
    late_slots = OWNERS * UNIT
    block_of = (iota((128, late_slots), 1) * 1366) >> 16
    order_col = order_of(iota((128, late_slots), 0), me)
    order_col = jnp.where(iota((128, late_slots), 0) < OWNERS, order_col, OWNERS)
    late_base = jnp.sum(dot(group_over, ones_where(order_col < block_of)), axis=0, keepdims=True)
    late_count = jnp.sum(dot(group_over, ones_where(order_col == block_of)), axis=0, keepdims=True)
    late_slot = (iota((1, late_slots), 1) - block_of[:1] * UNIT).astype(F32)
    late_row = jnp.where(late_slot < late_count, late_base + late_slot, -1.0)

    def gain_of(get, covers, lo, hi):
        for top in range(lo, hi, 64):
            end = min(top + 64, hi)
            part = acc[top:end]
            for k, cover in enumerate(covers):
                part += jnp.maximum(get(top, end, k) - cover, 0.0)
            acc[top:end] = part

    def one_pass(t, polls):
        lo, hi, step_rows = PASSES[t]
        groups = step_rows // 128

        def step(i, carry):
            at = pl.multiple_of(i * step_rows, step_rows)
            s = inner(ch[lo:hi], emb[pl.ds(at, step_rows), :])

            def kept(top, end, k):
                return raw[top:end, pl.ds(pl.multiple_of(at + 128 * k, 128), 128)]

            def new(top, end, k):
                return s[top - lo:end - lo, 128 * k:128 * k + 128]

            if t == 0:
                raw[:, pl.ds(at, step_rows)] = s
            elif t == 1:
                cover = jnp.max(s[:PICKS], axis=0, keepdims=True)
                covers = [cover[:, 128 * k:128 * k + 128] for k in range(groups)]
                for k in range(groups):
                    cover_ref[pl.ds(i * groups + k, 1), :] = covers[k]
                gain_of(kept, covers, 0, PICK_AT)
                gain_of(new, covers, PICK_AT + PICKS, hi)
            else:
                covers = [cover_ref[pl.ds(i * groups + k, 1), :] for k in range(groups)]
                gain_of(new, covers, lo, hi)
            for n, todo in polls.items():
                @pl.when(i == n)
                def _(todo=todo):
                    for act in todo:
                        act()
            return carry

        lax.fori_loop(0, rows // step_rows, step, 0)

    def in_place(lo, hi):
        found = jnp.sum(acc[lo:hi], axis=1, keepdims=True)
        row = (iota((hi - lo, 128), 0) + lo).astype(F32)
        parts = [
            jnp.sum(jnp.where(row == place[r:r + 1], found, 0.0), axis=0, keepdims=True) for r in range(8)
        ]
        return jnp.concatenate(parts, axis=0)

    def hand_all(part, chips):
        arrived(part, *evens(chips))
        for chip in chips:
            hand(part, chip).start()

    def near(part):
        arrived(part, *evens(NEAR))
        for dy in (1, 3):
            across(part, dy).start()
        relay(part, 0).start()
        for chip in NEAR:
            hand(part, chip).start()

    def diagonal(part):
        arrived(part, *evens(DIAG))
        if part not in STRAIGHT:
            relay(part, 1).start()
        for chip in DIAG:
            hand(part, chip).start()

    def send_late():
        for chip in NEAR:
            own(LATE, (*chip, 0)).start()
        own(LATE, SIB).start()
        if LATE in STRAIGHT:
            own(LATE, (*FAR[1], 0)).start()

    acc[...] = jnp.zeros((STREAM, 128), F32)
    pack[...] = ones_where(iota((REST, late_slots), 0).astype(F32) == late_row)
    arrived(CH, SLOT[SIB])
    one_pass(0, {2: [lambda: near(CH), send_late], 3: [lambda: hand_all(PK, NEAR + DIAG)]})
    hand_all(PK, FAR)
    arrived(CH, *odds(NEAR))
    arrived(PK, *range(1, OWNERS, 2))
    ch[PICK_AT:PICK_AT + PICKS] = dot(pick_pack, pk[...].reshape(OWNERS * PCAP, width)).astype(BF16)
    one_pass(1, {
        0: [lambda: diagonal(CH), lambda: hand_all(CH, FAR[:1]), lambda: near(LATE)],
        1: [lambda: hand_all(CH, FAR[1:]), lambda: hand_all(LATE, FAR[1:])],
    })
    cover_out.start()
    arrived(CH, *odds(DIAG + FAR[:1]))
    one_pass(2, {0: [lambda: diagonal(LATE), lambda: hand_all(LATE, FAR[:1])]})
    red[me] = in_place(0, PASSES[3][0])
    arrived(CH, *odds(FAR[1:]))
    arrived(LATE, *range(1, OWNERS, 2))
    packed = dot(pack[...], late[...].reshape(late_slots, width))
    ch[REST_AT:] = packed.astype(BF16)
    one_pass(3, {})

    red[me] += in_place(PASSES[3][0], STREAM)

    def share(rel, at):
        return remote(red.at[me], red.at[at], red_send.at[SLOT[rel]], red_recv.at[at], device(*rel))

    for rel in ORDER[:0:-1]:
        share(rel, me).start()
    for rel in ORDER[1:]:
        share(rel, device(*rel)).wait_recv()
    whole = red[0]
    for o in range(1, OWNERS):
        whole += red[o]
    gains_ref[...] = whole * (1.0 / (rows * OWNERS))

    cover_out.wait()
    for rel in ORDER[1:]:
        share(rel, me).wait_send()
    for part in (PK, CH, LATE):
        own(part, SIB).wait_send()
        for chip in NEAR + DIAG + FAR:
            if part is PK or chip in NEAR or (chip == FAR[1] and part in STRAIGHT):
                own(part, (*chip, 0)).wait_send()
            elif chip in DIAG:
                across(part, chip[1]).wait_send()
            else:
                relay(part, chip[0]).wait_send()
            hand(part, chip).wait_send()


def select_owned(embeddings, indices):
    count = embeddings.shape[0]
    local = indices - lax.axis_index("row") * count
    owned = (local >= 0) & (local < count)
    taken = jnp.take(embeddings, jnp.clip(local, 0, count - 1), axis=0)
    return jnp.where(owned[:, None], taken, jnp.zeros_like(taken))


def sum_over_rows(x):
    size = lax.axis_size("row")
    step = 1
    while step < size:
        x = x + lax.ppermute(x, "row", [(i, i ^ step) for i in range(size)])
        step *= 2
    return x


def whole_path(embeddings, pick_index, cand_index):
    count = embeddings.shape[0]
    per = cand_index.shape[0] // lax.axis_size("cand")
    mine = lax.dynamic_slice_in_dim(cand_index, lax.axis_index("cand") * per, per, 0)
    picked = sum_over_rows(select_owned(embeddings, pick_index))
    coverage = jnp.max(inner(embeddings, picked), axis=1)
    chosen = sum_over_rows(select_owned(embeddings, mine))
    similar = inner(embeddings, chosen)
    partial = jnp.sum(jnp.maximum(similar - coverage[:, None], 0.0), axis=0)
    return sum_over_rows(partial) / (count * lax.axis_size("row")), coverage


def settle(gains, cover, gains_out, cover_out, sem):
    copies = [
        pltpu.make_async_copy(gains, gains_out, sem.at[0]),
        pltpu.make_async_copy(cover, cover_out, sem.at[1]),
    ]
    for copy in copies:
        copy.start()
    for copy in copies:
        copy.wait()


def per_device(embeddings, pick_index, cand_index):
    rows, width = embeddings.shape
    shift = rows.bit_length() - 1
    chunks = 4
    anywhere = pl.BlockSpec(memory_space=pl.ANY)
    dma = pltpu.SemaphoreType.DMA
    gains, cover, flag = pl.pallas_call(
        functools.partial(kernel, shift),
        out_shape=[
            jax.ShapeDtypeStruct((8, 128), F32),
            jax.ShapeDtypeStruct((rows // 128, 128), F32),
            jax.ShapeDtypeStruct((1, 1), jnp.int32),
        ],
        in_specs=[anywhere, anywhere, anywhere],
        out_specs=[pl.BlockSpec(memory_space=pltpu.VMEM), anywhere, pl.BlockSpec(memory_space=pltpu.SMEM)],
        scratch_shapes=[
            pltpu.VMEM((64, 128), jnp.int32),
            pltpu.VMEM((1, PICKS), jnp.int32),
            pltpu.VMEM((rows, width), BF16),
            pltpu.VMEM((STREAM, width), BF16),
            pltpu.VMEM((OWNERS, UNIT, width), BF16),
            pltpu.VMEM((OWNERS, PCAP, width), BF16),
            pltpu.VMEM((REST, OWNERS * UNIT), BF16),
            pltpu.VMEM((PICK_AT, rows), F32),
            pltpu.VMEM((rows // 128, 128), F32),
            pltpu.VMEM((STREAM, 128), F32),
            pltpu.VMEM((OWNERS, 8, 128), F32),
            dma((3,)), dma((chunks,)),
        ] + [dma((OWNERS,))] * 8,
        compiler_params=pltpu.CompilerParams(
            collective_id=0, has_side_effects=True, vmem_limit_bytes=60 * 2**20),
        cost_estimate=pl.CostEstimate(
            flops=2 * rows * (PER + PICKS) * width, bytes_accessed=2 * rows * width, transcendentals=0),
    )(cand_index.reshape(-1, 128), pick_index.reshape(1, PICKS), embeddings)

    def fast_path():
        in_hbm = pl.BlockSpec(memory_space=pltpu.HBM)
        outs = pl.pallas_call(
            settle,
            out_shape=[jax.ShapeDtypeStruct(x.shape, F32) for x in (gains, cover)],
            in_specs=[anywhere] * 2, out_specs=[in_hbm] * 2, scratch_shapes=[dma((2,))],
        )(gains, cover)
        return outs[0].reshape(PER), outs[1].reshape(rows)

    return lax.cond(
        flag[0, 0] == 0, fast_path, lambda: whole_path(embeddings, pick_index, cand_index))


def solution(mesh):
    return jax.shard_map(
        per_device,
        mesh=mesh,
        in_specs=(P("row", None), P(), P()),
        out_specs=(P("cand"), P("row")),
        check_vma=False,
    )
```
